32 devices in a mesh: member: 2 (over x), mesh: 8 (over z, y), writer: 2 (over core).
Axes of the slice: x: 2, y: 2, z: 4, core: 2. Of those that a mesh axis runs over, the one named last changes fastest.
Arguments:
- mesh_nodes: bfloat16 [16384, 512], P(('member', 'mesh'), 'writer'), parts along dimension 0, may hold values from -6 to 6
- grid_state: bfloat16 [80, 131072], P(None, ('member', 'mesh', 'writer')), parts along dimension 1, may hold values from -6 to 6
- interp: bfloat16 [512, 4, 128, 128], P('mesh'), may hold values from -0.25 to 0.25
- wanted: int32 [8, 32], P('mesh'), may hold values from 0 to 63, as said below
- tile_slots: int32 [512, 4], P('mesh'), may hold values from 0 to 31
- edge_count: int32 [512], P('mesh'), may hold values from 1 to 4
- w_in: bfloat16 [512, 512], replicated, may hold values from -0.25 to 0.25
- b_in: bfloat16 [512], replicated, may hold values from -4 to 4
- w_out: bfloat16 [512, 80], replicated, may hold values from -0.25 to 0.25
- b_out: bfloat16 [80], replicated, may hold values from -2 to 2
- writer_order: int32 [80], replicated, may hold values from 0 to 79, each once
Outputs:
- written: bfloat16 [80, 131072], P('writer', ('member', 'mesh')), parts along dimension 1
The draws below stay inside these ranges and needn't reach their ends.
There are 2 independent parts, one for each index of `member`. The reference program is written for one: setup_inputs(seed, part) draws one part's arguments, and reference() takes and returns one part's arrays. A program takes and returns all parts, laid end to end along the dimension named above; an argument that names none is the same for every part. Nothing has to cross between parts.
Inputs may be any that keep to these rules, and one draw needn't show every extreme that they name: `wanted`: each row lists 32 different node blocks; at most 8 of them lie among the 8 blocks of one index of mesh, and exactly 8 do for one index, in every row.
All inputs are finite; a program needn't handle non-finite values.
Results may differ from the reference program's by a relative error of at most 0.0039.
Values may be sent and summed in bfloat16 or wider, within the bound.
No kernel may reach another device: no remote copies, remote signals or barrier semaphores. Data moves between devices by JAX's collectives and lax.ppermute only.
A program may use at most 128 MiB of HBM per device.

```python
import jax
import jax.numpy as jnp
from jax import lax

D = 512
CH = 80
BLK = 128
K = 4
TILES_DEV = 64
NB_DEV = 8
RQ = 32
CAP = 8
TILES = 512
POINTS = 65536
NODES = 8192
N_MESH = 8


def draw_wanted(key, part):
    key = jax.random.fold_in(key, 11)
    key_owner, key_offset = jax.random.split(key)
    scores = jax.random.randint(key_owner, (N_MESH, N_MESH), 0, 2 ** 20) * N_MESH + jnp.arange(N_MESH)[None, :]
    orders = jnp.argsort(scores, axis=1).astype(jnp.int32)
    slot_index = jnp.arange(RQ)
    position = jnp.where(slot_index < CAP, 0, 1 + (slot_index - CAP) % (N_MESH - 1))
    slot_rank = jnp.where(slot_index < CAP, slot_index, (slot_index - CAP) // (N_MESH - 1))
    owners = jnp.take_along_axis(orders, jnp.broadcast_to(position[None, :], (N_MESH, RQ)), axis=1)
    offsets = jax.random.randint(key_offset, (N_MESH, N_MESH), 0, NB_DEV)
    shifted = jnp.take_along_axis(offsets, owners, axis=1)
    local_ids = (shifted + slot_rank[None, :]) % NB_DEV
    return (owners * NB_DEV + local_ids).astype(jnp.int32)


def place_ends(result, stream_key, smallest, high):
    shape = result.shape
    index_at = [jax.random.randint(jax.random.fold_in(stream_key, axis), (), 0, shape[axis]) for axis in range(len(shape))]
    result = result.at[tuple(index_at)].set(smallest)
    longest = shape.index(max(shape))
    index_at[longest] = (index_at[longest] + 1) % shape[longest]
    return result.at[tuple(index_at)].set(high)


def steps_of(rng, dims, shards, least, top_value):
    factor_of, own = 1.0, jax.random.fold_in(rng, 6)
    for dim, blocks in shards:
        heights = jnp.exp(jax.random.uniform(jax.random.fold_in(own, dim), (blocks,), jnp.float32, least / len(shards), top_value / len(shards)))
        factor_of = factor_of * jnp.repeat(heights, dims[dim] // blocks).reshape([-1 if axis == dim else 1 for axis in range(len(dims))])
    return factor_of


def gaussian(stream_key, shape, deviation, bound, pieces=(), held_as=jnp.bfloat16):
    entries = deviation * jax.random.normal(stream_key, shape, jnp.float32)
    if pieces:
        entries = entries * steps_of(stream_key, shape, pieces, -0.22, 0.18)
    return jnp.clip(entries, -bound, bound).astype(held_as)


def setup_inputs(seed: int = 0, part: int = 0) -> dict:
    seeds = jax.random.split(jax.random.key(seed), 12)
    part_splits = jax.random.split(jax.random.fold_in(seeds[11], part), 12)
    return {
        "mesh_nodes": gaussian(part_splits[0], (NODES, D), 1.0, 6.0, ((0, 8), (1, 2))),
        "grid_state": gaussian(part_splits[1], (CH, POINTS), 1.0, 6.0, ((1, 16),)),
        "interp": gaussian(seeds[2], (TILES, K, BLK, BLK), (K * BLK) ** -0.5, 0.25, ((0, 8),)),
        "wanted": draw_wanted(jax.random.fold_in(seeds[11], 71), part),
        "tile_slots": place_ends(jax.random.randint(seeds[4], (TILES, K), 0, RQ), jax.random.fold_in(seeds[4], 1), 0, RQ - 1).astype(jnp.int32),
        "edge_count": place_ends(jax.random.randint(seeds[5], (TILES,), 1, K + 1), jax.random.fold_in(seeds[5], 1), 1, K).astype(jnp.int32),
        "w_in": gaussian(seeds[6], (D, D), D ** -0.5, 0.25),
        "b_in": gaussian(seeds[7], (D,), 1.0, 4.0),
        "w_out": gaussian(seeds[8], (D, CH), D ** -0.5, 0.25),
        "b_out": gaussian(seeds[9], (CH,), 0.5, 2.0),
        "writer_order": jax.random.permutation(seeds[10], CH).astype(jnp.int32),
    }


def reference(mesh_nodes, grid_state, interp, wanted, tile_slots, edge_count, w_in, b_in, w_out, b_out, writer_order):
    node_blocks = mesh_nodes.reshape(NODES // BLK, BLK, D)
    slots_all = tile_slots.reshape(N_MESH, TILES_DEV, K)
    counts_all = edge_count.reshape(N_MESH, TILES_DEV)
    interp_all = interp.reshape(N_MESH, TILES_DEV, K, BLK, BLK)

    def decode_part(items):
        block_list, slots, counts, weights = items
        listed = node_blocks[block_list].astype(jnp.float32)
        summed = jnp.zeros((TILES_DEV, BLK, D), jnp.float32)
        for slot_col in range(K):
            chosen = listed[slots[:, slot_col]]
            product = jnp.einsum("tpn,tnf->tpf", weights[:, slot_col].astype(jnp.float32), chosen, precision=lax.Precision.HIGHEST)
            live_mask = (slot_col < counts)[:, None, None]
            summed = summed + jnp.where(live_mask, product, jnp.float32(0.0))
        aggregated = summed.reshape(TILES_DEV * BLK, D).astype(jnp.bfloat16)
        layer_one = jnp.dot(aggregated, w_in, preferred_element_type=jnp.float32) + b_in.astype(jnp.float32)
        hidden = jax.nn.silu(layer_one).astype(jnp.bfloat16)
        return jnp.dot(hidden, w_out, preferred_element_type=jnp.float32) + b_out.astype(jnp.float32)

    decoded = lax.map(decode_part, (wanted, slots_all, counts_all, interp_all))
    decoded = decoded.reshape(POINTS, CH)
    combined = grid_state.astype(jnp.float32) + decoded.T
    return combined[writer_order].astype(jnp.bfloat16)
```

```python
import jax
import jax.numpy as jnp
from jax import lax
from jax.experimental import pallas as pl
from jax.experimental.pallas import tpu as pltpu
from jax.sharding import PartitionSpec as P

BLK = 128
K = 4
META = 8


def ring_position(index, count, columns):
    if columns == 1:
        return index
    row, column = index // 2, index % 2
    return jnp.where(column == 0, row, count - 1 - row)


def ring_order(count, columns):
    if columns == 1:
        return list(range(count))
    return list(range(0, count, 2)) + list(range(count - 1, 0, -2))


def decode_kernel(stage, blocks, pieces, tiles, *refs):
    meta, w_in, b_in, w_out, b_out, interp = refs[:6]
    piece_refs = refs[6 : 6 + 2 * len(pieces)]
    own_out, other_out, x_buf, a_buf, g_buf, o_buf, order, in_sem, out_sem = refs[
        8 + 2 * len(pieces) :
    ]
    half = piece_refs[0].shape[1]
    rows = own_out.shape[0]

    def columns_of(tile):
        return pl.ds(pl.multiple_of(tile * BLK, BLK), BLK)

    def grid_copies(tile, i):
        return [
            pltpu.make_async_copy(ref.at[:, columns_of(tile)], g_buf.at[i, pl.ds(j * rows, rows)], in_sem.at[i])
            for j, ref in enumerate((own_out, other_out))
        ]

    def out_copies(tile, i):
        return [
            pltpu.make_async_copy(o_buf.at[i, pl.ds(j * rows, rows)], ref.at[:, columns_of(tile)], out_sem)
            for j, ref in enumerate((own_out, other_out))
        ]

    def weight_copy(tile, i, k):
        return pltpu.make_async_copy(
            interp.at[meta[tile * META + K + 2], k], a_buf.at[i, :, pl.ds(k * BLK, BLK)], in_sem.at[i]
        )

    def node_copies(j, row, i, k):
        source = pl.ds(pl.multiple_of(row, BLK), BLK)
        return [
            pltpu.make_async_copy(
                piece_refs[2 * j + h].at[source],
                x_buf.at[i, pl.ds(k * BLK, BLK), pl.ds(h * half, half)],
                in_sem.at[i],
            )
            for h in range(2)
        ]

    def fetch(tile, i):
        live = meta[tile * META + K]
        for copy in grid_copies(tile, i):
            copy.start()
        for k in range(K):

            @pl.when(k < live)
            def _():
                weight_copy(tile, i, k).start()
                code = meta[tile * META + k]
                piece, row = code // blocks, (code % blocks) * BLK
                for j, where in enumerate(pieces):

                    @pl.when(piece == where)
                    def _():
                        for copy in node_copies(j, row, i, k):
                            copy.start()

            @pl.when(k >= live)
            def _():
                a_buf[i, :, k * BLK : (k + 1) * BLK] = jnp.zeros((BLK, BLK), jnp.bfloat16)
                x_buf[i, k * BLK : (k + 1) * BLK, :] = jnp.zeros((BLK, 2 * half), jnp.bfloat16)

    def arrive(i):
        tile = order[i]
        live = meta[tile * META + K]
        for copy in grid_copies(tile, i):
            copy.wait()
        for k in range(K):

            @pl.when(k < live)
            def _():
                weight_copy(tile, i, k).wait()
                for copy in node_copies(0, 0, i, k):
                    copy.wait()

    def scan(tile, count):
        mine = meta[tile * META + K + 1] == stage

        @pl.when(mine)
        def _():
            order[count] = tile
            fetch(tile, count)

        return count + mine.astype(jnp.int32)

    count = lax.fori_loop(0, tiles, scan, jnp.int32(0))

    def pair(g, _):
        for j in range(2):

            @pl.when(2 * g + j < count)
            def _():
                arrive(2 * g + j)

        aggregated = jnp.concatenate(
            [
                jnp.dot(a_buf[2 * g + j], x_buf[2 * g + j], preferred_element_type=jnp.float32).astype(jnp.bfloat16)
                for j in range(2)
            ],
            axis=0,
        )
        layer = jnp.dot(aggregated, w_in[...], preferred_element_type=jnp.float32) + b_in[...]
        hidden = (layer * (0.5 * jnp.tanh(0.5 * layer) + 0.5)).astype(jnp.bfloat16)
        decoded = lax.dot_general(
            w_out[...], hidden, (((1,), (1,)), ((), ())), preferred_element_type=jnp.float32
        )
        decoded = decoded + b_out[...]
        for j in range(2):
            i = 2 * g + j
            o_buf[i] = (g_buf[i].astype(jnp.float32) + decoded[:, j * BLK : (j + 1) * BLK]).astype(jnp.bfloat16)
        for j in range(2):

            @pl.when(2 * g + j < count)
            def _():
                for copy in out_copies(order[2 * g + j], 2 * g + j):
                    copy.start()

        return 0

    lax.fori_loop(0, (count + 1) // 2, pair, 0)

    def drain(i, _):
        for copy in out_copies(order[i], i):
            copy.wait()
        return 0

    lax.fori_loop(0, count, drain, 0)


def decode_tiles(stage, blocks, pieces, tiles, small, interp, arrays, outs):
    meta, w_in, b_in, w_out, b_out = small
    flat = [half for pair in arrays for half in pair]
    half = flat[0].shape[1]
    rows = outs[0].shape[0]
    vmem, anywhere = pl.BlockSpec(memory_space=pltpu.VMEM), pl.BlockSpec(memory_space=pl.ANY)
    first_out = 6 + len(flat)
    slots = tiles + tiles % 2
    share = max(tiles // 4, 1)
    return pl.pallas_call(
        lambda *refs: decode_kernel(stage, blocks, pieces, tiles, *refs),
        out_shape=[jax.ShapeDtypeStruct(out.shape, out.dtype) for out in outs],
        in_specs=[pl.BlockSpec(memory_space=pltpu.SMEM)] + [vmem] * 4 + [anywhere] * (1 + len(flat) + 2),
        out_specs=[anywhere] * 2,
        input_output_aliases={first_out: 0, first_out + 1: 1},
        scratch_shapes=[
            pltpu.VMEM((slots, K * BLK, 2 * half), jnp.bfloat16),
            pltpu.VMEM((slots, BLK, K * BLK), jnp.bfloat16),
            pltpu.VMEM((slots, 2 * rows, BLK), jnp.bfloat16),
            pltpu.VMEM((slots, 2 * rows, BLK), jnp.bfloat16),
            pltpu.SMEM((slots,), jnp.int32),
            pltpu.SemaphoreType.DMA((slots,)),
            pltpu.SemaphoreType.DMA,
        ],
        compiler_params=pltpu.CompilerParams(vmem_limit_bytes=48 * 2**20),
        cost_estimate=pl.CostEstimate(
            flops=share * BLK * 2 * (K * BLK * 2 * half + 4 * half * half + 4 * half * rows),
            bytes_accessed=share * 6 * BLK * BLK * 10,
            transcendentals=share * BLK * 2 * half,
        ),
        name="decode_tiles",
    )(meta, w_in, b_in, w_out, b_out, interp, *flat, *outs)


def make_local(count):
    columns = 2 if count == 8 else 1
    far = count // 2
    ring = ring_order(count, columns)
    onward = []
    for place in range(count):
        onward.append((ring[place] * 2, ring[(place + 1) % count] * 2))
        onward.append((ring[place] * 2 + 1, ring[(place - 1) % count] * 2 + 1))

    def send_on(piece):
        return lax.ppermute(piece, ("mesh", "writer"), onward)

    def swap(piece):
        return lax.ppermute(piece, "writer", [(0, 1), (1, 0)])

    def local(
        mesh_nodes,
        grid_state,
        interp,
        wanted,
        tile_slots,
        edge_count,
        w_in,
        b_in,
        w_out,
        b_out,
        writer_order,
    ):
        nodes, half = mesh_nodes.shape
        blocks = nodes // BLK
        core = lax.axis_index("writer")
        tiles = interp.shape[0] // 2
        channels = w_out.shape[1]
        each = channels // 2
        rows = -(-each // 16) * 16

        first_tile = core * tiles
        slots = lax.dynamic_slice_in_dim(tile_slots, first_tile, tiles, 0)
        live = lax.dynamic_slice_in_dim(edge_count, first_tile, tiles, 0)
        ids = wanted[0]
        here = ring_position(lax.axis_index("mesh"), count, columns)
        behind = here - ring_position(ids // blocks, count, columns)
        behind = jnp.mod(jnp.where(core == 0, behind, -behind), count)
        codes_listed = behind * blocks + ids % blocks
        chosen = slots[:, :, None] == jnp.arange(ids.shape[0])
        codes = jnp.sum(jnp.where(chosen, codes_listed, 0), axis=2)
        piece = codes // blocks
        distance = jnp.minimum(piece, count - piece)
        distance = jnp.max(jnp.where(jnp.arange(K) < live[:, None], distance, 0), axis=1)
        stages = [d for d in range(max(far - 3, 1), far + 1)]
        stage_of = jnp.maximum(distance, stages[0])
        numbers = first_tile + jnp.arange(tiles, dtype=jnp.int32)
        meta = jnp.concatenate(
            [codes, live[:, None], stage_of[:, None], numbers[:, None], jnp.zeros((tiles, 1), jnp.int32)], axis=1
        ).astype(jnp.int32).reshape(-1)

        weights = jnp.where(core == 0, w_in, jnp.roll(w_in, -half, axis=0))
        picks = jnp.where(core == 0, writer_order, jnp.roll(writer_order, -each))
        pad = jnp.broadcast_to(picks[:1], (rows - each,))
        picks = jnp.concatenate([picks[:each], pad, picks[each:], pad])
        heads = w_out.T[picks]
        head_bias = b_out.astype(jnp.float32)[picks][:, None]
        small = (meta, weights, b_in.astype(jnp.float32)[None], heads, head_bias)
        state = grid_state[picks]
        outs = [state[:rows], state[rows:]]

        other_nodes = swap(mesh_nodes)
        same, cross = [mesh_nodes], [other_nodes]
        table = {0: (mesh_nodes, other_nodes)}
        for d in range(1, far + 1):
            cross.append(send_on(cross[-1]))
            if d < far:
                same.append(send_on(same[-1]))
                table[d] = (same[d], cross[d])
                table[count - d] = (swap(cross[d]), swap(same[d]))
            else:
                table[d] = (swap(cross[d]), cross[d])
            if d in stages:
                pieces = sorted(table)
                outs = decode_tiles(
                    d, blocks, pieces, tiles, small, interp, [table[p] for p in pieces], outs
                )
        received = swap(outs[1])
        own, received = outs[0][:each], received[:each]
        return jnp.concatenate(
            [jnp.where(core == 0, own, received), jnp.where(core == 0, received, own)], axis=1
        )

    return local


def solution(mesh):
    placed = (
        P(("member", "mesh"), "writer"),
        P(None, ("member", "mesh", "writer")),
        P("mesh", None, None, None),
        P("mesh", None),
        P("mesh", None),
        P("mesh"),
        P(),
        P(),
        P(),
        P(),
        P(),
    )
    return jax.shard_map(
        make_local(mesh.shape["mesh"]),
        mesh=mesh,
        in_specs=placed,
        out_specs=P("writer", ("member", "mesh")),
        check_vma=False,
    )
```

```python
import jax
import jax.numpy as jnp
from jax import lax
from jax.experimental import pallas as pl
from jax.experimental.pallas import tpu as pltpu
from jax.sharding import PartitionSpec as P

BLK = 128
K = 4
GROUP = 4
META = 8


def ring_order(count, columns):
    if columns == 1:
        return list(range(count))
    return list(range(0, count, 2)) + list(range(count - 1, 0, -2))


def prepare_kernel(count, columns, blocks, wanted, slots, live, order, w_out, b_out, state, w_in, nodes, *rest):
    meta, heads, bias, ordered, w_in_kept, nodes_kept, codes, sem = rest
    kept = [
        pltpu.make_async_copy(source, target, sem.at[i])
        for i, (source, target) in enumerate([(w_in, w_in_kept), (nodes, nodes_kept)])
    ]
    for copy in kept:
        copy.start()
    core = lax.axis_index("writer")
    tiles = live.shape[0] // 2
    first_tile = core * tiles

    def place(index):
        if columns == 1:
            return index
        row = lax.shift_right_logical(index, 1)
        return jnp.where(lax.rem(index, 2) == 0, row, count - 1 - row)

    here = place(lax.axis_index("mesh"))
    first_stage = stages_of(count)[0]

    def locate(entry, _):
        block = wanted[0, entry]
        behind = here - place(lax.div(block, blocks))
        behind = jnp.where(core == 0, behind, -behind)
        behind = jnp.where(behind < 0, behind + count, behind)
        codes[entry] = behind * blocks + lax.rem(block, blocks)
        return 0

    lax.fori_loop(0, wanted.shape[1], locate, 0)
    stages = len(stages_of(count))
    for stage in range(stages):
        meta[tiles * META + stage * (tiles + 1)] = 0

    def describe(tile, _):
        number = first_tile + tile
        alive = live[number]
        stage = jnp.int32(first_stage)
        for k in range(K):
            code = codes[slots[k, number]]
            behind = lax.div(code, blocks)
            distance = jnp.minimum(behind, count - behind)
            stage = jnp.where(k < alive, jnp.maximum(stage, distance), stage)
            meta[tile * META + k] = code
        meta[tile * META + K] = alive
        meta[tile * META + K + 1] = number
        work = tiles * META + (stage - first_stage) * (tiles + 1)
        meta[work] = meta[work] + 1
        meta[work + meta[work]] = tile
        return 0

    lax.fori_loop(0, tiles, describe, 0)

    channels = state.shape[0]
    each = channels // 2
    rows = ordered.shape[0] // 2
    variable = lax.broadcasted_iota(jnp.int32, (channels, channels), 0)
    picks = jnp.where(variable == order[...], jnp.float32(1), jnp.float32(0)).T
    top, bottom = picks[:each], picks[each:]
    pad = jnp.zeros((rows - each, channels), jnp.float32)
    own, other = jnp.where(core == 0, top, bottom), jnp.where(core == 0, bottom, top)
    picks = jnp.concatenate([own, pad, other, pad], axis=0)
    bias[...] = jnp.sum(picks * b_out[...].astype(jnp.float32), axis=1, keepdims=True)
    picks = picks.astype(jnp.bfloat16)
    heads[...] = lax.dot_general(
        picks, w_out[...], (((1,), (0,)), ((), ())), preferred_element_type=jnp.float32
    ).astype(jnp.bfloat16)
    step = min(512, state.shape[1])
    for start in range(0, state.shape[1], step):
        part = jnp.dot(picks, state[:, start : start + step], preferred_element_type=jnp.float32)
        ordered[:, start : start + step] = part.astype(jnp.bfloat16)
    for copy in kept:
        copy.wait()


def in_hbm(array):
    return pltpu.with_memory_space_constraint(array, pltpu.HBM)


def prepare(count, columns, blocks, wanted, slots, live, order, w_out, b_out, state, w_in, nodes):
    vmem, smem = pl.BlockSpec(memory_space=pltpu.VMEM), pl.BlockSpec(memory_space=pltpu.SMEM)
    rows = 2 * (-(-(state.shape[0] // 2) // 16) * 16)
    tiles = live.shape[0] // 2
    return pl.pallas_call(
        lambda *refs: prepare_kernel(count, columns, blocks, *refs),
        out_shape=[
            jax.ShapeDtypeStruct((tiles * META + len(stages_of(count)) * (tiles + 1),), jnp.int32),
            jax.ShapeDtypeStruct((rows, w_out.shape[1]), jnp.bfloat16),
            jax.ShapeDtypeStruct((rows, 1), jnp.float32),
            jax.ShapeDtypeStruct((rows, state.shape[1]), jnp.bfloat16),
            jax.ShapeDtypeStruct(w_in.shape, w_in.dtype),
            jax.ShapeDtypeStruct(nodes.shape, nodes.dtype),
        ],
        in_specs=[smem] * 3 + [vmem] * 4 + [pl.BlockSpec(memory_space=pltpu.HBM)] * 2,
        out_specs=[smem] + [vmem] * 5,
        scratch_shapes=[pltpu.SMEM((wanted.shape[1],), jnp.int32), pltpu.SemaphoreType.DMA((2,))],
        compiler_params=pltpu.CompilerParams(vmem_limit_bytes=12 * 2**20),
        cost_estimate=pl.CostEstimate(flops=2 * rows * state.size, bytes_accessed=6 * state.size, transcendentals=0),
        name="prepare",
    )(*[in_hbm(x) for x in (wanted, slots, live, order, w_out, b_out, state, w_in, nodes)])


def stages_of(count):
    far = count // 2
    return list(range(max(far - 2, 1), far + 1))


def decode_kernel(stage, blocks, pieces, tiles, held, *refs):
    meta, w_in, b_in, w_out, b_out, state, interp = refs[:7]
    piece_refs = refs[7 : 7 + 2 * len(pieces)]
    own_out, other_out, x_buf, a_buf, in_sem = refs[7 + held + 2 * len(pieces) :]
    half = piece_refs[0].shape[1]
    rows = own_out.shape[0]
    core = lax.axis_index("writer")

    def columns_of(tile):
        return pl.ds(pl.multiple_of(tile * BLK, BLK), BLK)

    def weight_copy(tile, i):
        return pltpu.make_async_copy(interp.at[meta[tile * META + K + 1]], a_buf.at[i], in_sem.at[i])

    def take_block(code, j, k, low, high):
        if high - low > 1:
            middle = (low + high) // 2
            below = code < pieces[middle] * blocks
            pl.when(below)(lambda: take_block(code, j, k, low, middle))
            pl.when(jnp.logical_not(below))(lambda: take_block(code, j, k, middle, high))
            return
        source = pl.ds(pl.multiple_of((code - pieces[low] * blocks) * BLK, BLK), BLK)
        for h in range(2):
            x_buf[j, k * BLK : (k + 1) * BLK, h * half : (h + 1) * half] = piece_refs[2 * low + h][source, :]

    work = tiles * META + stage * (tiles + 1)
    count = meta[work]

    def tile_at(i):
        return meta[work + 1 + i]

    def fetch(i, _):
        weight_copy(tile_at(i), i).start()
        return 0

    lax.fori_loop(0, count, fetch, 0)

    def arrive(i, j):
        tile = tile_at(i)
        live = meta[tile * META + K]
        for k in range(K):

            @pl.when(k < live)
            def _():
                take_block(meta[tile * META + k], j, k, 0, len(pieces))

            @pl.when(k >= live)
            def _():
                x_buf[j, k * BLK : (k + 1) * BLK, :] = jnp.zeros((BLK, 2 * half), jnp.bfloat16)

        pltpu.make_async_copy(a_buf.at[i], a_buf.at[i], in_sem.at[i]).wait()

    def group(g, _):
        for j in range(GROUP):

            @pl.when(GROUP * g + j < count)
            def _():
                arrive(GROUP * g + j, j)

        aggregated = []
        for j in range(GROUP):
            i = GROUP * g + j
            spread = jnp.concatenate([a_buf[i, k] for k in range(K)], axis=1)
            aggregated.append(jnp.dot(spread, x_buf[j], preferred_element_type=jnp.float32).astype(jnp.bfloat16))
        aggregated = jnp.concatenate(aggregated, axis=0)
        layer = b_in[...].astype(jnp.float32)
        for h in range(2):
            features = pl.ds(pl.multiple_of((core if h == 0 else 1 - core) * half, half), half)
            layer = layer + jnp.dot(
                aggregated[:, h * half : (h + 1) * half], w_in[features, :], preferred_element_type=jnp.float32
            )
        hidden = (layer * (0.5 * jnp.tanh(0.5 * layer) + 0.5)).astype(jnp.bfloat16)
        decoded = lax.dot_general(
            w_out[...], hidden, (((1,), (1,)), ((), ())), preferred_element_type=jnp.float32
        )
        decoded = decoded + b_out[...]
        for j in range(GROUP):
            i = GROUP * g + j

            @pl.when(i < count)
            def _():
                tile = tile_at(i)
                before = state[:, columns_of(tile)].astype(jnp.float32)
                after = (before + decoded[:, j * BLK : (j + 1) * BLK]).astype(jnp.bfloat16)
                own_out[:, columns_of(tile)] = after[:rows]
                other_out[:, columns_of(tile)] = after[rows:]

        return 0

    lax.fori_loop(0, (count + GROUP - 1) // GROUP, group, 0)


def decode_tiles(stage, blocks, pieces, tiles, small, interp, arrays, outs):
    flat = [half for pair in arrays for half in pair]
    half = flat[0].shape[1]
    state = small[-1]
    rows = state.shape[0] // 2
    vmem = pl.BlockSpec(memory_space=pltpu.VMEM)
    first_out = 7 + len(flat)
    slots = -(-tiles // GROUP) * GROUP
    share = max(tiles // 4, 1)
    return pl.pallas_call(
        lambda *refs: decode_kernel(stage, blocks, pieces, tiles, len(outs), *refs),
        out_shape=[jax.ShapeDtypeStruct((rows, state.shape[1]), jnp.bfloat16)] * 2,
        in_specs=[pl.BlockSpec(memory_space=pltpu.SMEM)] + [vmem] * 5 + [pl.BlockSpec(memory_space=pltpu.HBM)] + [vmem] * (len(flat) + len(outs)),
        out_specs=[vmem] * 2,
        input_output_aliases={first_out + j: j for j in range(len(outs))},
        scratch_shapes=[
            pltpu.VMEM((GROUP, K * BLK, 2 * half), jnp.bfloat16),
            pltpu.VMEM((slots, K, BLK, BLK), jnp.bfloat16),
            pltpu.SemaphoreType.DMA((slots,)),
        ],
        compiler_params=pltpu.CompilerParams(vmem_limit_bytes=32 * 2**20),
        cost_estimate=pl.CostEstimate(
            flops=share * BLK * 2 * (K * BLK * 2 * half + 4 * half * half + 4 * half * rows),
            bytes_accessed=share * 6 * BLK * BLK * 10,
            transcendentals=share * BLK * 2 * half,
        ),
        name="decode_tiles",
    )(*small, in_hbm(interp), *flat, *outs)


def make_local(count):
    columns = 2 if count == 8 else 1
    far = count // 2
    ring = ring_order(count, columns)
    onward = []
    for place in range(count):
        onward.append((ring[place] * 2, ring[(place + 1) % count] * 2))
        onward.append((ring[place] * 2 + 1, ring[(place - 1) % count] * 2 + 1))

    def send_on(piece):
        return lax.ppermute(piece, ("mesh", "writer"), onward)

    def swap(piece):
        return lax.ppermute(piece, "writer", [(0, 1), (1, 0)])

    def local(
        mesh_nodes,
        grid_state,
        interp,
        wanted,
        tile_slots,
        edge_count,
        w_in,
        b_in,
        w_out,
        b_out,
        writer_order,
    ):
        nodes = mesh_nodes.shape[0]
        blocks = nodes // BLK
        core = lax.axis_index("writer")
        tiles = interp.shape[0] // 2
        each = w_out.shape[1] // 2
        stages = stages_of(count)
        meta, heads, bias, state, w_in, nodes_kept = prepare(
            count,
            columns,
            blocks,
            wanted,
            tile_slots.T,
            edge_count,
            writer_order[None],
            w_out.T,
            b_out[None],
            grid_state,
            w_in,
            mesh_nodes,
        )
        small = (meta, w_in, b_in[None], heads, bias, state)
        outs = []

        other_nodes = swap(mesh_nodes)
        same, cross = [mesh_nodes], [other_nodes]
        table = {0: (nodes_kept, other_nodes)}
        def decode(d, outs):
            pieces = [p for p in sorted(table) if min(p, count - p) <= d]
            return list(
                decode_tiles(stages.index(d), blocks, pieces, tiles, small, interp, [table[p] for p in pieces], outs)
            )

        for d in range(1, far + 1):
            if d == 2:
                same[-1], small = lax.optimization_barrier((same[-1], small))
            if outs:
                same[-1], outs = lax.optimization_barrier((same[-1], outs))
            same.append(send_on(same[-1]))
            if d < far:
                cross.append(send_on(cross[-1]))
                table[d] = (same[d], cross[d])
                table[count - d] = (swap(cross[d]), swap(same[d]))
            else:
                table[d] = (same[d], swap(same[d]))
            if d - 1 in stages:
                outs = decode(d - 1, outs)
        outs = decode(far, outs)
        received = swap(outs[1])
        own, received = outs[0][:each], received[:each]
        return jnp.concatenate(
            [jnp.where(core == 0, own, received), jnp.where(core == 0, received, own)], axis=1
        )

    return local


def solution(mesh):
    placed = (
        P(("member", "mesh"), "writer"),
        P(None, ("member", "mesh", "writer")),
        P("mesh", None, None, None),
        P("mesh", None),
        P("mesh", None),
        P("mesh"),
        P(),
        P(),
        P(),
        P(),
        P(),
    )
    return jax.shard_map(
        make_local(mesh.shape["mesh"]),
        mesh=mesh,
        in_specs=placed,
        out_specs=P("writer", ("member", "mesh")),
        check_vma=False,
    )
```

```python
import jax
import jax.numpy as jnp
from jax import lax
from jax.experimental import pallas as pl
from jax.experimental.pallas import tpu as pltpu
from jax.sharding import PartitionSpec as P

BLK = 128
K = 4
GROUP = 4
META = 8


def ring_order(count, columns):
    if columns == 1:
        return list(range(count))
    return list(range(0, count, 2)) + list(range(count - 1, 0, -2))


def prepare_kernel(count, columns, blocks, wanted, slots, live, order, w_out, b_out, state, w_in, nodes, interp, *rest):
    meta, heads, bias, ordered, w_in_kept, nodes_kept, interp_kept, codes, sem = rest
    core = lax.axis_index("writer")
    tiles = live.shape[0] // 2
    first_tile = core * tiles
    pairs = [(w_in, w_in_kept), (nodes, nodes_kept)]
    eighth = max(tiles // 8, 1)
    for start in range(0, tiles, eighth):
        pairs.append((interp.at[pl.ds(first_tile + start, eighth)], interp_kept.at[pl.ds(start, eighth)]))
    kept = [pltpu.make_async_copy(source, target, sem.at[i]) for i, (source, target) in enumerate(pairs)]
    for copy in kept:
        copy.start()

    def place(index):
        if columns == 1:
            return index
        row = lax.shift_right_logical(index, 1)
        return jnp.where(lax.rem(index, 2) == 0, row, count - 1 - row)

    here = place(lax.axis_index("mesh"))
    first_stage = stages_of(count)[0]

    def locate(entry, _):
        block = wanted[0, entry]
        behind = here - place(lax.div(block, blocks))
        behind = jnp.where(core == 0, behind, -behind)
        behind = jnp.where(behind < 0, behind + count, behind)
        codes[entry] = behind * blocks + lax.rem(block, blocks)
        return 0

    lax.fori_loop(0, wanted.shape[1], locate, 0)
    stages = len(stages_of(count))
    for stage in range(stages):
        meta[tiles * META + stage * (tiles + 1)] = 0

    def describe(tile, _):
        number = first_tile + tile
        alive = live[number]
        stage = jnp.int32(first_stage)
        for k in range(K):
            code = codes[slots[k, number]]
            behind = lax.div(code, blocks)
            distance = jnp.minimum(behind, count - behind)
            stage = jnp.where(k < alive, jnp.maximum(stage, distance), stage)
            meta[tile * META + k] = code
        meta[tile * META + K] = alive
        meta[tile * META + K + 1] = number
        work = tiles * META + (stage - first_stage) * (tiles + 1)
        meta[work] = meta[work] + 1
        meta[work + meta[work]] = tile
        return 0

    lax.fori_loop(0, tiles, describe, 0)

    channels = state.shape[0]
    each = channels // 2
    rows = ordered.shape[0] // 2
    variable = lax.broadcasted_iota(jnp.int32, (channels, channels), 0)
    picks = jnp.where(variable == order[...], jnp.float32(1), jnp.float32(0)).T
    top, bottom = picks[:each], picks[each:]
    pad = jnp.zeros((rows - each, channels), jnp.float32)
    own, other = jnp.where(core == 0, top, bottom), jnp.where(core == 0, bottom, top)
    picks = jnp.concatenate([own, pad, other, pad], axis=0)
    bias[...] = jnp.sum(picks * b_out[...].astype(jnp.float32), axis=1, keepdims=True)
    picks = picks.astype(jnp.bfloat16)
    heads[...] = lax.dot_general(
        picks, w_out[...], (((1,), (0,)), ((), ())), preferred_element_type=jnp.float32
    ).astype(jnp.bfloat16)
    step = min(512, state.shape[1])
    for start in range(0, state.shape[1], step):
        part = jnp.dot(picks, state[:, start : start + step], preferred_element_type=jnp.float32)
        ordered[:, start : start + step] = part.astype(jnp.bfloat16)
    for copy in kept:
        copy.wait()


def in_hbm(array):
    return pltpu.with_memory_space_constraint(array, pltpu.HBM)


def prepare(count, columns, blocks, wanted, slots, live, order, w_out, b_out, state, w_in, nodes, interp):
    vmem, smem = pl.BlockSpec(memory_space=pltpu.VMEM), pl.BlockSpec(memory_space=pltpu.SMEM)
    rows = 2 * (-(-(state.shape[0] // 2) // 16) * 16)
    tiles = live.shape[0] // 2
    return pl.pallas_call(
        lambda *refs: prepare_kernel(count, columns, blocks, *refs),
        out_shape=[
            jax.ShapeDtypeStruct((tiles * META + len(stages_of(count)) * (tiles + 1),), jnp.int32),
            jax.ShapeDtypeStruct((rows, w_out.shape[1]), jnp.bfloat16),
            jax.ShapeDtypeStruct((rows, 1), jnp.float32),
            jax.ShapeDtypeStruct((rows, state.shape[1]), jnp.bfloat16),
            jax.ShapeDtypeStruct(w_in.shape, w_in.dtype),
            jax.ShapeDtypeStruct(nodes.shape, nodes.dtype),
            jax.ShapeDtypeStruct((tiles, *interp.shape[1:]), interp.dtype),
        ],
        in_specs=[smem] * 3 + [vmem] * 4 + [pl.BlockSpec(memory_space=pltpu.HBM)] * 3,
        out_specs=[smem] + [vmem] * 6,
        scratch_shapes=[pltpu.SMEM((wanted.shape[1],), jnp.int32), pltpu.SemaphoreType.DMA((2 + min(tiles, 8),))],
        compiler_params=pltpu.CompilerParams(vmem_limit_bytes=12 * 2**20),
        cost_estimate=pl.CostEstimate(flops=2 * rows * state.size, bytes_accessed=6 * state.size, transcendentals=0),
        name="prepare",
    )(*[in_hbm(x) for x in (wanted, slots, live, order, w_out, b_out, state, w_in, nodes, interp)])


def stages_of(count):
    far = count // 2
    return list(range(max(far - 2, 1), far + 1))


def decode_kernel(stage, blocks, pieces, tiles, held, *refs):
    meta, w_in, b_in, w_out, b_out, state, interp = refs[:7]
    piece_refs = refs[7 : 7 + 2 * len(pieces)]
    own_out, other_out, x_buf = refs[7 + held + 2 * len(pieces) :]
    half = piece_refs[0].shape[1]
    rows = own_out.shape[0]
    core = lax.axis_index("writer")

    def columns_of(tile):
        return pl.ds(pl.multiple_of(tile * BLK, BLK), BLK)

    def take_block(code, j, k, low, high):
        if high - low > 1:
            middle = (low + high) // 2
            below = code < pieces[middle] * blocks
            pl.when(below)(lambda: take_block(code, j, k, low, middle))
            pl.when(jnp.logical_not(below))(lambda: take_block(code, j, k, middle, high))
            return
        source = pl.ds(pl.multiple_of((code - pieces[low] * blocks) * BLK, BLK), BLK)
        for h in range(2):
            x_buf[j, k * BLK : (k + 1) * BLK, h * half : (h + 1) * half] = piece_refs[2 * low + h][source, :]

    work = tiles * META + stage * (tiles + 1)
    count = meta[work]

    def tile_at(i):
        return meta[work + 1 + i]

    def arrive(i, j):
        tile = tile_at(i)
        live = meta[tile * META + K]
        for k in range(K):

            @pl.when(k < live)
            def _():
                take_block(meta[tile * META + k], j, k, 0, len(pieces))

            @pl.when(k >= live)
            def _():
                x_buf[j, k * BLK : (k + 1) * BLK, :] = jnp.zeros((BLK, 2 * half), jnp.bfloat16)

    def group(g, _):
        for j in range(GROUP):

            @pl.when(GROUP * g + j < count)
            def _():
                arrive(GROUP * g + j, j)

        aggregated = []
        for j in range(GROUP):
            tile = tile_at(jnp.minimum(GROUP * g + j, count - 1))
            spread = jnp.concatenate([interp[tile, k] for k in range(K)], axis=1)
            aggregated.append(jnp.dot(spread, x_buf[j], preferred_element_type=jnp.float32).astype(jnp.bfloat16))
        aggregated = jnp.concatenate(aggregated, axis=0)
        layer = b_in[...].astype(jnp.float32)
        for h in range(2):
            features = pl.ds(pl.multiple_of((core if h == 0 else 1 - core) * half, half), half)
            layer = layer + jnp.dot(
                aggregated[:, h * half : (h + 1) * half], w_in[features, :], preferred_element_type=jnp.float32
            )
        hidden = (layer * (0.5 * jnp.tanh(0.5 * layer) + 0.5)).astype(jnp.bfloat16)
        decoded = lax.dot_general(
            w_out[...], hidden, (((1,), (1,)), ((), ())), preferred_element_type=jnp.float32
        )
        decoded = decoded + b_out[...]
        for j in range(GROUP):
            i = GROUP * g + j

            @pl.when(i < count)
            def _():
                tile = tile_at(i)
                before = state[:, columns_of(tile)].astype(jnp.float32)
                after = (before + decoded[:, j * BLK : (j + 1) * BLK]).astype(jnp.bfloat16)
                own_out[:, columns_of(tile)] = after[:rows]
                other_out[:, columns_of(tile)] = after[rows:]

        return 0

    lax.fori_loop(0, (count + GROUP - 1) // GROUP, group, 0)


def decode_tiles(stage, blocks, pieces, tiles, small, arrays, outs):
    flat = [half for pair in arrays for half in pair]
    half = flat[0].shape[1]
    state = small[-2]
    rows = state.shape[0] // 2
    vmem = pl.BlockSpec(memory_space=pltpu.VMEM)
    first_out = 7 + len(flat)
    share = max(tiles // 4, 1)
    return pl.pallas_call(
        lambda *refs: decode_kernel(stage, blocks, pieces, tiles, len(outs), *refs),
        out_shape=[jax.ShapeDtypeStruct((rows, state.shape[1]), jnp.bfloat16)] * 2,
        in_specs=[pl.BlockSpec(memory_space=pltpu.SMEM)] + [vmem] * (6 + len(flat) + len(outs)),
        out_specs=[vmem] * 2,
        input_output_aliases={first_out + j: j for j in range(len(outs))},
        scratch_shapes=[pltpu.VMEM((GROUP, K * BLK, 2 * half), jnp.bfloat16)],
        compiler_params=pltpu.CompilerParams(vmem_limit_bytes=16 * 2**20),
        cost_estimate=pl.CostEstimate(
            flops=share * BLK * 2 * (K * BLK * 2 * half + 4 * half * half + 4 * half * rows),
            bytes_accessed=share * 6 * BLK * BLK * 10,
            transcendentals=share * BLK * 2 * half,
        ),
        name="decode_tiles",
    )(*small, *flat, *outs)


def make_local(count):
    columns = 2 if count == 8 else 1
    far = count // 2
    ring = ring_order(count, columns)
    onward = []
    for place in range(count):
        onward.append((ring[place] * 2, ring[(place + 1) % count] * 2))
        onward.append((ring[place] * 2 + 1, ring[(place - 1) % count] * 2 + 1))

    def send_on(piece):
        return lax.ppermute(piece, ("mesh", "writer"), onward)

    def swap(piece):
        return lax.ppermute(piece, "writer", [(0, 1), (1, 0)])

    def local(
        mesh_nodes,
        grid_state,
        interp,
        wanted,
        tile_slots,
        edge_count,
        w_in,
        b_in,
        w_out,
        b_out,
        writer_order,
    ):
        nodes = mesh_nodes.shape[0]
        blocks = nodes // BLK
        core = lax.axis_index("writer")
        tiles = interp.shape[0] // 2
        each = w_out.shape[1] // 2
        stages = stages_of(count)
        meta, heads, bias, state, w_in, nodes_kept, interp_kept = prepare(
            count,
            columns,
            blocks,
            wanted,
            tile_slots.T,
            edge_count,
            writer_order[None],
            w_out.T,
            b_out[None],
            grid_state,
            w_in,
            mesh_nodes,
            interp,
        )
        small = (meta, w_in, b_in[None], heads, bias, state, interp_kept)
        outs = []

        other_nodes = swap(mesh_nodes)
        same, cross = [mesh_nodes], [other_nodes]
        table = {0: (nodes_kept, other_nodes)}
        def decode(d, outs):
            pieces = [p for p in sorted(table) if min(p, count - p) <= d]
            return list(
                decode_tiles(stages.index(d), blocks, pieces, tiles, small, [table[p] for p in pieces], outs)
            )

        for d in range(1, far + 1):
            if d == 2:
                same[-1], small = lax.optimization_barrier((same[-1], small))
            same.append(send_on(same[-1]))
            if d < far:
                cross.append(send_on(cross[-1]))
            swapped = (cross[-1], same[-1])
            if d - 1 in stages:
                outs = decode(d - 1, outs)
                if d < far:
                    *swapped, outs = lax.optimization_barrier((*swapped, outs))
            if d < far:
                table[d] = (same[d], cross[d])
                table[count - d] = (swap(swapped[0]), swap(swapped[1]))
            else:
                table[d] = (same[d], swap(swapped[1]))
        outs = decode(far, outs)
        received = swap(outs[1])
        own, received = outs[0][:each], received[:each]
        return jnp.concatenate(
            [jnp.where(core == 0, own, received), jnp.where(core == 0, received, own)], axis=1
        )

    return local


def solution(mesh):
    placed = (
        P(("member", "mesh"), "writer"),
        P(None, ("member", "mesh", "writer")),
        P("mesh", None, None, None),
        P("mesh", None),
        P("mesh", None),
        P("mesh"),
        P(),
        P(),
        P(),
        P(),
        P(),
    )
    return jax.shard_map(
        make_local(mesh.shape["mesh"]),
        mesh=mesh,
        in_specs=placed,
        out_specs=P("writer", ("member", "mesh")),
        check_vma=False,
    )
```

```python
import jax
import jax.numpy as jnp
from jax import lax
from jax.experimental import pallas as pl
from jax.experimental.pallas import tpu as pltpu
from jax.sharding import PartitionSpec as P

BLK = 128
K = 4
GROUP = 8
META = 5


def ring_order(count, columns):
    if columns == 1:
        return list(range(count))
    return list(range(0, count, 2)) + list(range(count - 1, 0, -2))


def prepare_kernel(count, columns, blocks, wanted, slots, live, order, w_out, b_out, state, w_in, nodes, interp, *rest):
    meta, heads, bias, ordered, w_in_kept, nodes_kept, interp_kept, entry_stage, sem = rest
    core = lax.axis_index("writer")
    tiles = live.shape[0] // 2
    first_tile = core * tiles
    pairs = [(w_in, w_in_kept), (nodes, nodes_kept)]
    eighth = max(tiles // 8, 1)
    for start in range(0, tiles, eighth):
        pairs.append((interp.at[pl.ds(first_tile + start, eighth)], interp_kept.at[pl.ds(start, eighth)]))
    kept = [pltpu.make_async_copy(source, target, sem.at[i]) for i, (source, target) in enumerate(pairs)]
    for copy in kept:
        copy.start()

    def place(index):
        if columns == 1:
            return index
        row = lax.shift_right_logical(index, 1)
        return jnp.where(lax.rem(index, 2) == 0, row, count - 1 - row)

    here = place(lax.axis_index("mesh"))
    first_stage = stages_of(count)[0]

    listed = wanted.shape[1]
    entry_work = tiles * META + len(stages_of(count)) * (tiles + 1)
    for stage in range(len(stages_of(count))):
        meta[tiles * META + stage * (tiles + 1)] = 0
        meta[entry_work + stage * (listed + 1)] = 0

    def locate(entry, _):
        block = wanted[0, entry]
        behind = here - place(lax.div(block, blocks))
        behind = jnp.where(core == 0, behind, -behind)
        behind = jnp.where(behind < 0, behind + count, behind)
        stage = jnp.maximum(jnp.minimum(behind, count - behind), first_stage) - first_stage
        entry_stage[entry] = stage
        work = entry_work + stage * (listed + 1)
        meta[work] = meta[work] + 1
        code = behind * blocks + lax.rem(block, blocks)
        meta[work + meta[work]] = code * listed + entry
        return 0

    lax.fori_loop(0, listed, locate, 0)

    def describe(tile, _):
        number = first_tile + tile
        alive = live[number]
        stage = jnp.int32(0)
        for k in range(K):
            entry = slots[jnp.where(k < alive, k, 0), number]
            stage = jnp.maximum(stage, entry_stage[entry])
            meta[tile * META + k] = entry
        meta[tile * META + K] = alive
        work = tiles * META + stage * (tiles + 1)
        meta[work] = meta[work] + 1
        meta[work + meta[work]] = tile
        return 0

    lax.fori_loop(0, tiles, describe, 0)

    channels = state.shape[0]
    each = channels // 2
    rows = ordered.shape[0] // 2
    variable = lax.broadcasted_iota(jnp.int32, (channels, channels), 0)
    picks = jnp.where(variable == order[...], jnp.float32(1), jnp.float32(0)).T
    top, bottom = picks[:each], picks[each:]
    pad = jnp.zeros((rows - each, channels), jnp.float32)
    own, other = jnp.where(core == 0, top, bottom), jnp.where(core == 0, bottom, top)
    picks = jnp.concatenate([own, pad, other, pad], axis=0)
    bias[...] = jnp.sum(picks * b_out[...].astype(jnp.float32), axis=1, keepdims=True)
    picks = picks.astype(jnp.bfloat16)
    heads[...] = lax.dot_general(
        picks, w_out[...], (((1,), (0,)), ((), ())), preferred_element_type=jnp.float32
    ).astype(jnp.bfloat16)
    step = min(512, state.shape[1])
    for start in range(0, state.shape[1], step):
        part = jnp.dot(picks, state[:, start : start + step], preferred_element_type=jnp.float32)
        ordered[:, start : start + step] = part.astype(jnp.bfloat16)
    for copy in kept:
        copy.wait()


def in_hbm(array):
    return pltpu.with_memory_space_constraint(array, pltpu.HBM)


def prepare(count, columns, blocks, wanted, slots, live, order, w_out, b_out, state, w_in, nodes, interp):
    vmem, smem = pl.BlockSpec(memory_space=pltpu.VMEM), pl.BlockSpec(memory_space=pltpu.SMEM)
    rows = 2 * (-(-(state.shape[0] // 2) // 16) * 16)
    tiles = live.shape[0] // 2
    return pl.pallas_call(
        lambda *refs: prepare_kernel(count, columns, blocks, *refs),
        out_shape=[
            jax.ShapeDtypeStruct((tiles * META + len(stages_of(count)) * (tiles + wanted.shape[1] + 2),), jnp.int32),
            jax.ShapeDtypeStruct((rows, w_out.shape[1]), jnp.bfloat16),
            jax.ShapeDtypeStruct((rows, 1), jnp.float32),
            jax.ShapeDtypeStruct((rows, state.shape[1]), jnp.bfloat16),
            jax.ShapeDtypeStruct(w_in.shape, w_in.dtype),
            jax.ShapeDtypeStruct(nodes.shape, nodes.dtype),
            jax.ShapeDtypeStruct((tiles, *interp.shape[1:]), interp.dtype),
        ],
        in_specs=[smem] * 3 + [vmem] * 4 + [pl.BlockSpec(memory_space=pltpu.HBM)] * 3,
        out_specs=[smem] + [vmem] * 6,
        scratch_shapes=[pltpu.SMEM((wanted.shape[1],), jnp.int32), pltpu.SemaphoreType.DMA((2 + min(tiles, 8),))],
        compiler_params=pltpu.CompilerParams(vmem_limit_bytes=12 * 2**20),
        cost_estimate=pl.CostEstimate(flops=2 * rows * state.size, bytes_accessed=6 * state.size, transcendentals=0),
        name="prepare",
    )(*[in_hbm(x) for x in (wanted, slots, live, order, w_out, b_out, state, w_in, nodes, interp)])


def stages_of(count):
    far = count // 2
    return list(range(max(far - 2, 1), far + 1))


def decode_kernel(stage, stages, blocks, pieces, tiles, held, *refs):
    meta, w_in, b_in, w_out, b_out, state, interp = refs[:7]
    piece_refs = refs[7 : 7 + 2 * len(pieces)]
    own_out, other_out, found = refs[7 + held + 2 * len(pieces) :]
    half = piece_refs[0].shape[1]
    rows = own_out.shape[0]
    listed = found.shape[0]
    core = lax.axis_index("writer")

    def columns_of(tile):
        return pl.ds(pl.multiple_of(tile * BLK, BLK), BLK)

    def take_block(code, entry, low, high):
        if high - low > 1:
            middle = (low + high) // 2
            below = code < pieces[middle] * blocks
            pl.when(below)(lambda: take_block(code, entry, low, middle))
            pl.when(jnp.logical_not(below))(lambda: take_block(code, entry, middle, high))
            return
        source = pl.ds(pl.multiple_of((code - pieces[low] * blocks) * BLK, BLK), BLK)
        for h in range(2):
            found[entry, :, h * half : (h + 1) * half] = piece_refs[2 * low + h][source, :]

    fresh = tiles * META + stages * (tiles + 1) + stage * (listed + 1)

    def take(i, _):
        packed = meta[fresh + 1 + i]
        take_block(lax.div(packed, listed), lax.rem(packed, listed), 0, len(pieces))
        return 0

    lax.fori_loop(0, meta[fresh], take, 0)

    work = tiles * META + stage * (tiles + 1)
    count = meta[work]

    def tile_at(i):
        return meta[work + 1 + i]

    def decode(first, size):
        aggregated = []
        for j in range(size):
            tile = tile_at(jnp.minimum(first + j, count - 1))
            live = meta[tile * META + K]
            spread = [interp[tile, k] for k in range(K)]
            spread = [a if k == 0 else jnp.where(k < live, a, jnp.zeros_like(a)) for k, a in enumerate(spread)]
            nodes = [found[meta[tile * META + k]] for k in range(K)]
            total = jnp.dot(
                jnp.concatenate(spread, axis=1), jnp.concatenate(nodes, axis=0), preferred_element_type=jnp.float32
            )
            aggregated.append(total.astype(jnp.bfloat16))
        aggregated = jnp.concatenate(aggregated, axis=0)
        layer = b_in[...].astype(jnp.float32)
        for h in range(2):
            features = pl.ds(pl.multiple_of((core if h == 0 else 1 - core) * half, half), half)
            layer = layer + jnp.dot(
                aggregated[:, h * half : (h + 1) * half], w_in[features, :], preferred_element_type=jnp.float32
            )
        hidden = (layer * (0.5 * jnp.tanh(0.5 * layer) + 0.5)).astype(jnp.bfloat16)
        decoded = lax.dot_general(
            w_out[...], hidden, (((1,), (1,)), ((), ())), preferred_element_type=jnp.float32
        )
        decoded = decoded + b_out[...]
        for j in range(size):
            i = first + j

            @pl.when(i < count)
            def _():
                tile = tile_at(i)
                before = state[:, columns_of(tile)].astype(jnp.float32)
                after = (before + decoded[:, j * BLK : (j + 1) * BLK]).astype(jnp.bfloat16)
                own_out[:, columns_of(tile)] = after[:rows]
                other_out[:, columns_of(tile)] = after[rows:]

    def large(g, _):
        decode(g * GROUP, GROUP)
        return 0

    groups = (count + GROUP // 2 - 1) // GROUP
    lax.fori_loop(0, groups, large, 0)

    @pl.when(groups * GROUP < count)
    def _():
        decode(groups * GROUP, GROUP // 2)


def decode_tiles(stage, stages, blocks, pieces, tiles, listed, small, arrays, outs):
    flat = [half for pair in arrays for half in pair]
    half = flat[0].shape[1]
    state = small[-2]
    rows = state.shape[0] // 2
    vmem = pl.BlockSpec(memory_space=pltpu.VMEM)
    first_out = 7 + len(flat)
    share = max(tiles // 4, 1)
    return pl.pallas_call(
        lambda *refs: decode_kernel(stage, stages, blocks, pieces, tiles, len(outs), *refs),
        out_shape=[jax.ShapeDtypeStruct((rows, state.shape[1]), jnp.bfloat16)] * 2
        + [jax.ShapeDtypeStruct((listed, BLK, 2 * half), jnp.bfloat16)],
        in_specs=[pl.BlockSpec(memory_space=pltpu.SMEM)] + [vmem] * (6 + len(flat) + len(outs)),
        out_specs=[vmem] * 3,
        input_output_aliases={first_out + j: j for j in range(len(outs))},
        compiler_params=pltpu.CompilerParams(vmem_limit_bytes=16 * 2**20),
        cost_estimate=pl.CostEstimate(
            flops=share * BLK * 2 * (K * BLK * 2 * half + 4 * half * half + 4 * half * rows),
            bytes_accessed=share * 6 * BLK * BLK * 10,
            transcendentals=share * BLK * 2 * half,
        ),
        name="decode_tiles",
    )(*small, *flat, *outs)


def make_local(count):
    columns = 2 if count == 8 else 1
    far = count // 2
    ring = ring_order(count, columns)
    onward = []
    for place in range(count):
        onward.append((ring[place] * 2, ring[(place + 1) % count] * 2))
        onward.append((ring[place] * 2 + 1, ring[(place - 1) % count] * 2 + 1))

    def send_on(piece):
        return lax.ppermute(piece, ("mesh", "writer"), onward)

    def swap(piece):
        return lax.ppermute(piece, "writer", [(0, 1), (1, 0)])

    def local(
        mesh_nodes,
        grid_state,
        interp,
        wanted,
        tile_slots,
        edge_count,
        w_in,
        b_in,
        w_out,
        b_out,
        writer_order,
    ):
        nodes = mesh_nodes.shape[0]
        blocks = nodes // BLK
        core = lax.axis_index("writer")
        tiles = interp.shape[0] // 2
        each = w_out.shape[1] // 2
        stages = stages_of(count)
        meta, heads, bias, state, w_in, nodes_kept, interp_kept = prepare(
            count,
            columns,
            blocks,
            wanted,
            tile_slots.T,
            edge_count,
            writer_order[None],
            w_out.T,
            b_out[None],
            grid_state,
            w_in,
            mesh_nodes,
            interp,
        )
        small = (meta, w_in, b_in[None], heads, bias, state, interp_kept)
        outs = []

        other_nodes = swap(mesh_nodes)
        same, cross = [mesh_nodes], [other_nodes]
        table = {0: (nodes_kept, other_nodes)}
        def decode(d, outs):
            distances = range(d + 1) if d == stages[0] else (d,)
            pieces = [p for p in sorted(table) if min(p, count - p) in distances]
            return list(
                decode_tiles(
                    stages.index(d),
                    len(stages),
                    blocks,
                    pieces,
                    tiles,
                    wanted.shape[1],
                    small,
                    [table[p] for p in pieces],
                    outs,
                )
            )

        for d in range(1, far + 1):
            if d == 2:
                same[-1], small = lax.optimization_barrier((same[-1], small))
            same.append(send_on(same[-1]))
            if d < far:
                cross.append(send_on(cross[-1]))
            swapped = (cross[-1], same[-1])
            if d - 1 in stages:
                outs = decode(d - 1, outs)
                if d < far:
                    *swapped, outs = lax.optimization_barrier((*swapped, outs))
            if d < far:
                table[d] = (same[d], cross[d])
                table[count - d] = (swap(swapped[0]), swap(swapped[1]))
            else:
                table[d] = (same[d], swap(swapped[1]))
        outs = decode(far, outs)
        received = swap(outs[1])
        own, received = outs[0][:each], received[:each]
        return jnp.concatenate(
            [jnp.where(core == 0, own, received), jnp.where(core == 0, received, own)], axis=1
        )

    return local


def solution(mesh):
    placed = (
        P(("member", "mesh"), "writer"),
        P(None, ("member", "mesh", "writer")),
        P("mesh", None, None, None),
        P("mesh", None),
        P("mesh", None),
        P("mesh"),
        P(),
        P(),
        P(),
        P(),
        P(),
    )
    return jax.shard_map(
        make_local(mesh.shape["mesh"]),
        mesh=mesh,
        in_specs=placed,
        out_specs=P("writer", ("member", "mesh")),
        check_vma=False,
    )
```

```python
import jax
import jax.numpy as jnp
from jax import lax
from jax.experimental import pallas as pl
from jax.experimental.pallas import tpu as pltpu
from jax.sharding import PartitionSpec as P

BLK = 128
K = 4
GROUP = 8
META = 5


def ring_order(count, columns):
    if columns == 1:
        return list(range(count))
    return list(range(0, count, 2)) + list(range(count - 1, 0, -2))


def prepare_kernel(count, columns, blocks, wanted, slots, live, order, w_out, b_out, state, w_in, nodes, interp, *rest):
    meta, heads, bias, ordered, w_in_kept, nodes_kept, interp_kept, entry_stage, sem = rest
    core = lax.axis_index("writer")
    tiles = live.shape[0] // 2
    first_tile = core * tiles
    pairs = [(w_in, w_in_kept), (nodes, nodes_kept)]
    eighth = max(tiles // 8, 1)
    for start in range(0, tiles, eighth):
        pairs.append((interp.at[pl.ds(first_tile + start, eighth)], interp_kept.at[pl.ds(start, eighth)]))
    kept = [pltpu.make_async_copy(source, target, sem.at[i]) for i, (source, target) in enumerate(pairs)]
    for copy in kept:
        copy.start()

    def place(index):
        if columns == 1:
            return index
        row = lax.shift_right_logical(index, 1)
        return jnp.where(lax.rem(index, 2) == 0, row, count - 1 - row)

    here = place(lax.axis_index("mesh"))
    first_stage = stages_of(count)[0]

    listed = wanted.shape[1]
    entry_work = tiles * META + len(stages_of(count)) * (tiles + 1)
    for stage in range(len(stages_of(count))):
        meta[tiles * META + stage * (tiles + 1)] = 0
        meta[entry_work + stage * (listed + 1)] = 0

    def locate(entry, _):
        block = wanted[0, entry]
        behind = here - place(lax.div(block, blocks))
        behind = jnp.where(core == 0, behind, -behind)
        behind = jnp.where(behind < 0, behind + count, behind)
        stage = jnp.maximum(jnp.minimum(behind, count - behind), first_stage) - first_stage
        entry_stage[entry] = stage
        work = entry_work + stage * (listed + 1)
        meta[work] = meta[work] + 1
        code = behind * blocks + lax.rem(block, blocks)
        meta[work + meta[work]] = code * listed + entry
        return 0

    lax.fori_loop(0, listed, locate, 0)

    def describe(tile, _):
        number = first_tile + tile
        alive = live[number]
        stage = jnp.int32(0)
        for k in range(K):
            entry = slots[jnp.where(k < alive, k, 0), number]
            stage = jnp.maximum(stage, entry_stage[entry])
            meta[tile * META + k] = entry
        meta[tile * META + K] = alive
        work = tiles * META + stage * (tiles + 1)
        meta[work] = meta[work] + 1
        meta[work + meta[work]] = tile
        return 0

    lax.fori_loop(0, tiles, describe, 0)

    channels = state.shape[0]
    each = channels // 2
    rows = ordered.shape[0] // 2
    variable = lax.broadcasted_iota(jnp.int32, (channels, channels), 0)
    picks = jnp.where(variable == order[...], jnp.float32(1), jnp.float32(0)).T
    top, bottom = picks[:each], picks[each:]
    pad = jnp.zeros((rows - each, channels), jnp.float32)
    own, other = jnp.where(core == 0, top, bottom), jnp.where(core == 0, bottom, top)
    picks = jnp.concatenate([own, pad, other, pad], axis=0)
    bias[...] = jnp.sum(picks * b_out[...].astype(jnp.float32), axis=1, keepdims=True)
    picks = picks.astype(jnp.bfloat16)
    heads[...] = lax.dot_general(
        picks, w_out[...], (((1,), (0,)), ((), ())), preferred_element_type=jnp.float32
    ).astype(jnp.bfloat16)
    step = min(512, state.shape[1])
    for start in range(0, state.shape[1], step):
        part = jnp.dot(picks, state[:, start : start + step], preferred_element_type=jnp.float32)
        ordered[:, start : start + step] = part.astype(jnp.bfloat16)
    for copy in kept:
        copy.wait()


def in_hbm(array):
    return pltpu.with_memory_space_constraint(array, pltpu.HBM)


def prepare(count, columns, blocks, wanted, slots, live, order, w_out, b_out, state, w_in, nodes, interp):
    vmem, smem = pl.BlockSpec(memory_space=pltpu.VMEM), pl.BlockSpec(memory_space=pltpu.SMEM)
    rows = 2 * (-(-(state.shape[0] // 2) // 16) * 16)
    tiles = live.shape[0] // 2
    return pl.pallas_call(
        lambda *refs: prepare_kernel(count, columns, blocks, *refs),
        out_shape=[
            jax.ShapeDtypeStruct((tiles * META + len(stages_of(count)) * (tiles + wanted.shape[1] + 2),), jnp.int32),
            jax.ShapeDtypeStruct((rows, w_out.shape[1]), jnp.bfloat16),
            jax.ShapeDtypeStruct((rows, 1), jnp.float32),
            jax.ShapeDtypeStruct((rows, state.shape[1]), jnp.bfloat16),
            jax.ShapeDtypeStruct(w_in.shape, w_in.dtype),
            jax.ShapeDtypeStruct(nodes.shape, nodes.dtype),
            jax.ShapeDtypeStruct((tiles, *interp.shape[1:]), interp.dtype),
        ],
        in_specs=[smem] * 3 + [vmem] * 4 + [pl.BlockSpec(memory_space=pltpu.HBM)] * 3,
        out_specs=[smem] + [vmem] * 6,
        scratch_shapes=[pltpu.SMEM((wanted.shape[1],), jnp.int32), pltpu.SemaphoreType.DMA((2 + min(tiles, 8),))],
        compiler_params=pltpu.CompilerParams(vmem_limit_bytes=12 * 2**20),
        cost_estimate=pl.CostEstimate(flops=2 * rows * state.size, bytes_accessed=6 * state.size, transcendentals=0),
        name="prepare",
    )(*[in_hbm(x) for x in (wanted, slots, live, order, w_out, b_out, state, w_in, nodes, interp)])


def stages_of(count):
    far = count // 2
    return list(range(max(far - 3, 1), far + 1))


def decode_kernel(stage, stages, blocks, pieces, tiles, held, *refs):
    meta, w_in, b_in, w_out, b_out, state, interp = refs[:7]
    piece_refs = refs[7 : 7 + 2 * len(pieces)]
    own_out, other_out, found = refs[7 + held + 2 * len(pieces) :]
    half = piece_refs[0].shape[1]
    rows = own_out.shape[0]
    listed = found.shape[0]
    core = lax.axis_index("writer")

    def columns_of(tile):
        return pl.ds(pl.multiple_of(tile * BLK, BLK), BLK)

    def take_block(code, entry, low, high):
        if high - low > 1:
            middle = (low + high) // 2
            below = code < pieces[middle] * blocks
            pl.when(below)(lambda: take_block(code, entry, low, middle))
            pl.when(jnp.logical_not(below))(lambda: take_block(code, entry, middle, high))
            return
        source = pl.ds(pl.multiple_of((code - pieces[low] * blocks) * BLK, BLK), BLK)
        for h in range(2):
            found[entry, :, h * half : (h + 1) * half] = piece_refs[2 * low + h][source, :]

    fresh = tiles * META + stages * (tiles + 1) + stage * (listed + 1)

    def take(i, _):
        packed = meta[fresh + 1 + i]
        take_block(lax.div(packed, listed), lax.rem(packed, listed), 0, len(pieces))
        return 0

    lax.fori_loop(0, meta[fresh], take, 0)

    work = tiles * META + stage * (tiles + 1)
    count = meta[work]

    def tile_at(i):
        return meta[work + 1 + i]

    def decode(first, size):
        aggregated = []
        for j in range(size):
            tile = tile_at(jnp.minimum(first + j, count - 1))
            live = meta[tile * META + K]
            spread = [interp[tile, k] for k in range(K)]
            spread = [a if k == 0 else jnp.where(k < live, a, jnp.zeros_like(a)) for k, a in enumerate(spread)]
            nodes = [found[meta[tile * META + k]] for k in range(K)]
            total = jnp.dot(
                jnp.concatenate(spread, axis=1), jnp.concatenate(nodes, axis=0), preferred_element_type=jnp.float32
            )
            aggregated.append(total.astype(jnp.bfloat16))
        aggregated = jnp.concatenate(aggregated, axis=0)
        layer = b_in[...].astype(jnp.float32)
        for h in range(2):
            features = pl.ds(pl.multiple_of((core if h == 0 else 1 - core) * half, half), half)
            layer = layer + jnp.dot(
                aggregated[:, h * half : (h + 1) * half], w_in[features, :], preferred_element_type=jnp.float32
            )
        hidden = (layer * (0.5 * jnp.tanh(0.5 * layer) + 0.5)).astype(jnp.bfloat16)
        decoded = lax.dot_general(
            w_out[...], hidden, (((1,), (1,)), ((), ())), preferred_element_type=jnp.float32
        )
        decoded = decoded + b_out[...]
        for j in range(size):
            tile = tile_at(jnp.minimum(first + j, count - 1))
            before = state[:, columns_of(tile)].astype(jnp.float32)
            after = (before + decoded[:, j * BLK : (j + 1) * BLK]).astype(jnp.bfloat16)
            own_out[:, columns_of(tile)] = after[:rows]
            other_out[:, columns_of(tile)] = after[rows:]

    def large(g, _):
        decode(g * GROUP, GROUP)
        return 0

    groups = (count + GROUP // 2 - 1) // GROUP
    lax.fori_loop(0, groups, large, 0)

    @pl.when(groups * GROUP < count)
    def _():
        decode(groups * GROUP, GROUP // 2)


def decode_tiles(stage, stages, blocks, pieces, tiles, listed, small, arrays, outs):
    flat = [half for pair in arrays for half in pair]
    half = flat[0].shape[1]
    state = small[-2]
    rows = state.shape[0] // 2
    vmem = pl.BlockSpec(memory_space=pltpu.VMEM)
    first_out = 7 + len(flat)
    share = max(tiles // 4, 1)
    return pl.pallas_call(
        lambda *refs: decode_kernel(stage, stages, blocks, pieces, tiles, len(outs), *refs),
        out_shape=[jax.ShapeDtypeStruct((rows, state.shape[1]), jnp.bfloat16)] * 2
        + [jax.ShapeDtypeStruct((listed, BLK, 2 * half), jnp.bfloat16)],
        in_specs=[pl.BlockSpec(memory_space=pltpu.SMEM)] + [vmem] * (6 + len(flat) + len(outs)),
        out_specs=[vmem] * 3,
        input_output_aliases={first_out + j: j for j in range(len(outs))},
        compiler_params=pltpu.CompilerParams(vmem_limit_bytes=16 * 2**20),
        cost_estimate=pl.CostEstimate(
            flops=share * BLK * 2 * (K * BLK * 2 * half + 4 * half * half + 4 * half * rows),
            bytes_accessed=share * 6 * BLK * BLK * 10,
            transcendentals=share * BLK * 2 * half,
        ),
        name="decode_tiles",
    )(*small, *flat, *outs)


def make_local(count):
    columns = 2 if count == 8 else 1
    far = count // 2
    ring = ring_order(count, columns)
    onward = []
    for place in range(count):
        onward.append((ring[place] * 2, ring[(place + 1) % count] * 2))
        onward.append((ring[place] * 2 + 1, ring[(place - 1) % count] * 2 + 1))

    def send_on(piece):
        return lax.ppermute(piece, ("mesh", "writer"), onward)

    def swap(piece):
        return lax.ppermute(piece, "writer", [(0, 1), (1, 0)])

    def local(
        mesh_nodes,
        grid_state,
        interp,
        wanted,
        tile_slots,
        edge_count,
        w_in,
        b_in,
        w_out,
        b_out,
        writer_order,
    ):
        nodes = mesh_nodes.shape[0]
        blocks = nodes // BLK
        core = lax.axis_index("writer")
        tiles = interp.shape[0] // 2
        each = w_out.shape[1] // 2
        stages = stages_of(count)
        meta, heads, bias, state, w_in, nodes_kept, interp_kept = prepare(
            count,
            columns,
            blocks,
            wanted,
            tile_slots.T,
            edge_count,
            writer_order[None],
            w_out.T,
            b_out[None],
            grid_state,
            w_in,
            mesh_nodes,
            interp,
        )
        small = (meta, w_in, b_in[None], heads, bias, state, interp_kept)
        outs = []

        other_nodes = swap(mesh_nodes)
        same, cross = [mesh_nodes], [other_nodes]
        table = {0: (nodes_kept, other_nodes)}
        def decode(d, outs):
            distances = range(d + 1) if d == stages[0] else (d,)
            pieces = [p for p in sorted(table) if min(p, count - p) in distances]
            return list(
                decode_tiles(
                    stages.index(d),
                    len(stages),
                    blocks,
                    pieces,
                    tiles,
                    wanted.shape[1],
                    small,
                    [table[p] for p in pieces],
                    outs,
                )
            )

        for d in range(1, far + 1):
            if d == 2:
                same[-1], small = lax.optimization_barrier((same[-1], small))
            same.append(send_on(same[-1]))
            if d < far:
                cross.append(send_on(cross[-1]))
            swapped = (cross[-1], same[-1])
            if d - 1 in stages:
                outs = decode(d - 1, outs)
                if d < far:
                    *swapped, outs = lax.optimization_barrier((*swapped, outs))
            if d < far:
                table[d] = (same[d], cross[d])
                table[count - d] = (swap(swapped[0]), swap(swapped[1]))
            else:
                table[d] = (same[d], swap(swapped[1]))
        outs = decode(far, outs)
        received = swap(outs[1])
        own, received = outs[0][:each], received[:each]
        return jnp.concatenate(
            [jnp.where(core == 0, own, received), jnp.where(core == 0, received, own)], axis=1
        )

    return local


def solution(mesh):
    placed = (
        P(("member", "mesh"), "writer"),
        P(None, ("member", "mesh", "writer")),
        P("mesh", None, None, None),
        P("mesh", None),
        P("mesh", None),
        P("mesh"),
        P(),
        P(),
        P(),
        P(),
        P(),
    )
    return jax.shard_map(
        make_local(mesh.shape["mesh"]),
        mesh=mesh,
        in_specs=placed,
        out_specs=P("writer", ("member", "mesh")),
        check_vma=False,
    )
```

```python
import jax
import jax.numpy as jnp
from jax import lax
from jax.experimental import pallas as pl
from jax.experimental.pallas import tpu as pltpu
from jax.sharding import PartitionSpec as P

BLK = 128
K = 4
GROUP = 8
META = 5


def ring_order(count, columns):
    if columns == 1:
        return list(range(count))
    return list(range(0, count, 2)) + list(range(count - 1, 0, -2))


def prepare_kernel(count, columns, blocks, wanted, slots, live, order, w_out, b_out, state, w_in, nodes, interp, *rest):
    meta, heads, bias, ordered, w_in_kept, nodes_kept, interp_kept, entry_stage, sem = rest
    core = lax.axis_index("writer")
    tiles = live.shape[0] // 2
    first_tile = core * tiles
    pairs = [(w_in, w_in_kept), (nodes, nodes_kept)]
    eighth = max(tiles // 8, 1)
    for start in range(0, tiles, eighth):
        pairs.append((interp.at[pl.ds(first_tile + start, eighth)], interp_kept.at[pl.ds(start, eighth)]))
    kept = [pltpu.make_async_copy(source, target, sem.at[i]) for i, (source, target) in enumerate(pairs)]
    for copy in kept:
        copy.start()

    def place(index):
        if columns == 1:
            return index
        row = lax.shift_right_logical(index, 1)
        return jnp.where(lax.rem(index, 2) == 0, row, count - 1 - row)

    here = place(lax.axis_index("mesh"))
    first_stage = stages_of(count)[0]

    listed = wanted.shape[1]
    entry_work = tiles * META + len(levels_of(count)) * (tiles + 1)
    for stage in range(len(levels_of(count))):
        meta[tiles * META + stage * (tiles + 1)] = 0
        meta[entry_work + stage * (listed + 1)] = 0

    def locate(entry, _):
        block = wanted[0, entry]
        behind = here - place(lax.div(block, blocks))
        behind = jnp.where(core == 0, behind, -behind)
        behind = jnp.where(behind < 0, behind + count, behind)
        distance = jnp.minimum(behind, count - behind)
        stage = jnp.maximum(distance, first_stage) - first_stage
        far = count // 2
        if first_stage < far - 1:
            second = jnp.logical_or(distance == far, jnp.logical_and(distance == far - 1, behind > far))
            stage = stage + second.astype(jnp.int32)
        entry_stage[entry] = stage
        work = entry_work + stage * (listed + 1)
        meta[work] = meta[work] + 1
        code = behind * blocks + lax.rem(block, blocks)
        meta[work + meta[work]] = code * listed + entry
        return 0

    lax.fori_loop(0, listed, locate, 0)

    def describe(tile, _):
        number = first_tile + tile
        alive = live[number]
        stage = jnp.int32(0)
        for k in range(K):
            entry = slots[jnp.where(k < alive, k, 0), number]
            stage = jnp.maximum(stage, entry_stage[entry])
            meta[tile * META + k] = entry
        meta[tile * META + K] = alive
        work = tiles * META + stage * (tiles + 1)
        meta[work] = meta[work] + 1
        meta[work + meta[work]] = tile
        return 0

    lax.fori_loop(0, tiles, describe, 0)

    channels = state.shape[0]
    each = channels // 2
    rows = ordered.shape[0] // 2
    variable = lax.broadcasted_iota(jnp.int32, (channels, channels), 0)
    picks = jnp.where(variable == order[...], jnp.float32(1), jnp.float32(0)).T
    top, bottom = picks[:each], picks[each:]
    pad = jnp.zeros((rows - each, channels), jnp.float32)
    own, other = jnp.where(core == 0, top, bottom), jnp.where(core == 0, bottom, top)
    picks = jnp.concatenate([own, pad, other, pad], axis=0)
    bias[...] = jnp.sum(picks * b_out[...].astype(jnp.float32), axis=1, keepdims=True)
    picks = picks.astype(jnp.bfloat16)
    heads[...] = lax.dot_general(
        picks, w_out[...], (((1,), (0,)), ((), ())), preferred_element_type=jnp.float32
    ).astype(jnp.bfloat16)
    step = min(512, state.shape[1])
    for start in range(0, state.shape[1], step):
        part = jnp.dot(picks, state[:, start : start + step], preferred_element_type=jnp.float32)
        ordered[:, start : start + step] = part.astype(jnp.bfloat16)
    for copy in kept:
        copy.wait()


def in_hbm(array):
    return pltpu.with_memory_space_constraint(array, pltpu.HBM)


def prepare(count, columns, blocks, wanted, slots, live, order, w_out, b_out, state, w_in, nodes, interp):
    vmem, smem = pl.BlockSpec(memory_space=pltpu.VMEM), pl.BlockSpec(memory_space=pltpu.SMEM)
    rows = 2 * (-(-(state.shape[0] // 2) // 16) * 16)
    tiles = live.shape[0] // 2
    return pl.pallas_call(
        lambda *refs: prepare_kernel(count, columns, blocks, *refs),
        out_shape=[
            jax.ShapeDtypeStruct((tiles * META + len(levels_of(count)) * (tiles + wanted.shape[1] + 2),), jnp.int32),
            jax.ShapeDtypeStruct((rows, w_out.shape[1]), jnp.bfloat16),
            jax.ShapeDtypeStruct((rows, 1), jnp.float32),
            jax.ShapeDtypeStruct((rows, state.shape[1]), jnp.bfloat16),
            jax.ShapeDtypeStruct(w_in.shape, w_in.dtype),
            jax.ShapeDtypeStruct(nodes.shape, nodes.dtype),
            jax.ShapeDtypeStruct((tiles, *interp.shape[1:]), interp.dtype),
        ],
        in_specs=[smem] * 3 + [vmem] * 4 + [pl.BlockSpec(memory_space=pltpu.HBM)] * 3,
        out_specs=[smem] + [vmem] * 6,
        scratch_shapes=[pltpu.SMEM((wanted.shape[1],), jnp.int32), pltpu.SemaphoreType.DMA((2 + min(tiles, 8),))],
        compiler_params=pltpu.CompilerParams(vmem_limit_bytes=12 * 2**20),
        cost_estimate=pl.CostEstimate(flops=2 * rows * state.size, bytes_accessed=6 * state.size, transcendentals=0),
        name="prepare",
    )(*[in_hbm(x) for x in (wanted, slots, live, order, w_out, b_out, state, w_in, nodes, interp)])


def stages_of(count):
    far = count // 2
    return list(range(max(far - 3, 1), far + 1))


def levels_of(count):
    far, levels = count // 2, []
    for d in stages_of(count):
        if d == stages_of(count)[0]:
            levels.append([p for p in range(count) if min(p, count - p) <= d])
        elif d == far - 1:
            levels += [[d], [count - d]]
        else:
            levels.append(sorted({d, count - d}))
    return levels


def decode_kernel(stage, stages, blocks, pieces, tiles, held, *refs):
    meta, w_in, b_in, w_out, b_out, state, interp = refs[:7]
    piece_refs = refs[7 : 7 + 2 * len(pieces)]
    own_out, other_out, found = refs[7 + held + 2 * len(pieces) :]
    half = piece_refs[0].shape[1]
    rows = own_out.shape[0]
    listed = found.shape[0]
    core = lax.axis_index("writer")

    def columns_of(tile):
        return pl.ds(pl.multiple_of(tile * BLK, BLK), BLK)

    def take_block(code, entry, low, high):
        if high - low > 1:
            middle = (low + high) // 2
            below = code < pieces[middle] * blocks
            pl.when(below)(lambda: take_block(code, entry, low, middle))
            pl.when(jnp.logical_not(below))(lambda: take_block(code, entry, middle, high))
            return
        source = pl.ds(pl.multiple_of((code - pieces[low] * blocks) * BLK, BLK), BLK)
        for h in range(2):
            found[entry, :, h * half : (h + 1) * half] = piece_refs[2 * low + h][source, :]

    fresh = tiles * META + stages * (tiles + 1) + stage * (listed + 1)

    def take(i, _):
        packed = meta[fresh + 1 + i]
        take_block(lax.div(packed, listed), lax.rem(packed, listed), 0, len(pieces))
        return 0

    lax.fori_loop(0, meta[fresh], take, 0)

    work = tiles * META + stage * (tiles + 1)
    count = meta[work]

    def tile_at(i):
        return meta[work + 1 + i]

    def decode(first, size):
        aggregated = []
        for j in range(size):
            tile = tile_at(jnp.minimum(first + j, count - 1))
            live = meta[tile * META + K]
            spread = [interp[tile, k] for k in range(K)]
            spread = [a if k == 0 else jnp.where(k < live, a, jnp.zeros_like(a)) for k, a in enumerate(spread)]
            nodes = [found[meta[tile * META + k]] for k in range(K)]
            total = jnp.dot(
                jnp.concatenate(spread, axis=1), jnp.concatenate(nodes, axis=0), preferred_element_type=jnp.float32
            )
            aggregated.append(total.astype(jnp.bfloat16))
        aggregated = jnp.concatenate(aggregated, axis=0)
        layer = b_in[...].astype(jnp.float32)
        for h in range(2):
            features = pl.ds(pl.multiple_of((core if h == 0 else 1 - core) * half, half), half)
            layer = layer + jnp.dot(
                aggregated[:, h * half : (h + 1) * half], w_in[features, :], preferred_element_type=jnp.float32
            )
        hidden = (layer * (0.5 * jnp.tanh(0.5 * layer) + 0.5)).astype(jnp.bfloat16)
        decoded = lax.dot_general(
            w_out[...], hidden, (((1,), (1,)), ((), ())), preferred_element_type=jnp.float32
        )
        decoded = decoded + b_out[...]
        for j in range(size):
            tile = tile_at(jnp.minimum(first + j, count - 1))
            before = state[:, columns_of(tile)].astype(jnp.float32)
            after = (before + decoded[:, j * BLK : (j + 1) * BLK]).astype(jnp.bfloat16)
            own_out[:, columns_of(tile)] = after[:rows]
            other_out[:, columns_of(tile)] = after[rows:]

    def large(g, _):
        decode(g * GROUP, GROUP)
        return 0

    groups = (count + GROUP // 2 - 1) // GROUP
    lax.fori_loop(0, groups, large, 0)

    @pl.when(groups * GROUP < count)
    def _():
        decode(groups * GROUP, GROUP // 2)


def decode_tiles(stage, stages, blocks, pieces, tiles, listed, small, arrays, outs):
    flat = [half for pair in arrays for half in pair]
    half = flat[0].shape[1]
    state = small[-2]
    rows = state.shape[0] // 2
    vmem = pl.BlockSpec(memory_space=pltpu.VMEM)
    first_out = 7 + len(flat)
    share = max(tiles // 4, 1)
    return pl.pallas_call(
        lambda *refs: decode_kernel(stage, stages, blocks, pieces, tiles, len(outs), *refs),
        out_shape=[jax.ShapeDtypeStruct((rows, state.shape[1]), jnp.bfloat16)] * 2
        + [jax.ShapeDtypeStruct((listed, BLK, 2 * half), jnp.bfloat16)],
        in_specs=[pl.BlockSpec(memory_space=pltpu.SMEM)] + [vmem] * (6 + len(flat) + len(outs)),
        out_specs=[vmem] * 3,
        input_output_aliases={first_out + j: j for j in range(len(outs))},
        compiler_params=pltpu.CompilerParams(vmem_limit_bytes=16 * 2**20),
        cost_estimate=pl.CostEstimate(
            flops=share * BLK * 2 * (K * BLK * 2 * half + 4 * half * half + 4 * half * rows),
            bytes_accessed=share * 6 * BLK * BLK * 10,
            transcendentals=share * BLK * 2 * half,
        ),
        name="decode_tiles",
    )(*small, *flat, *outs)


def make_local(count):
    columns = 2 if count == 8 else 1
    far = count // 2
    ring = ring_order(count, columns)
    onward = []
    for place in range(count):
        onward.append((ring[place] * 2, ring[(place + 1) % count] * 2))
        onward.append((ring[place] * 2 + 1, ring[(place - 1) % count] * 2 + 1))

    def send_on(piece):
        return lax.ppermute(piece, ("mesh", "writer"), onward)

    def swap(piece):
        return lax.ppermute(piece, "writer", [(0, 1), (1, 0)])

    def local(
        mesh_nodes,
        grid_state,
        interp,
        wanted,
        tile_slots,
        edge_count,
        w_in,
        b_in,
        w_out,
        b_out,
        writer_order,
    ):
        nodes = mesh_nodes.shape[0]
        blocks = nodes // BLK
        core = lax.axis_index("writer")
        tiles = interp.shape[0] // 2
        each = w_out.shape[1] // 2
        stages, levels = stages_of(count), levels_of(count)
        meta, heads, bias, state, w_in, nodes_kept, interp_kept = prepare(
            count,
            columns,
            blocks,
            wanted,
            tile_slots.T,
            edge_count,
            writer_order[None],
            w_out.T,
            b_out[None],
            grid_state,
            w_in,
            mesh_nodes,
            interp,
        )
        small = (meta, w_in, b_in[None], heads, bias, state, interp_kept)
        outs = []

        other_nodes = swap(mesh_nodes)
        same, cross = [mesh_nodes], [other_nodes]
        table = {0: (nodes_kept, other_nodes)}
        def decode(level, outs):
            pieces = levels[level]
            return list(
                decode_tiles(
                    level,
                    len(levels),
                    blocks,
                    pieces,
                    tiles,
                    wanted.shape[1],
                    small,
                    [table[p] for p in pieces],
                    outs,
                )
            )

        level = 0
        for d in range(1, far):
            if d == 2:
                same[-1], small = lax.optimization_barrier((same[-1], small))
            same.append(send_on(same[-1]))
            cross.append(send_on(cross[-1]))
            table[d] = (same[d], cross[d])
            swapped = (cross[d], same[d])
            if d - 1 in stages:
                outs, level = decode(level, outs), level + 1
                if d == far - 1:
                    last, outs = lax.optimization_barrier((same[d], outs))
                    outs, level = decode(level, outs), level + 1
                    first, outs = lax.optimization_barrier((cross[d], outs))
                    swapped = (first, last)
                else:
                    *swapped, outs = lax.optimization_barrier((*swapped, outs))
            table[count - d] = (swap(swapped[0]), swap(swapped[1]))
        same.append(send_on(same[-1]))
        outs = decode(level, outs)
        table[far] = (same[far], swap(same[far]))
        outs = decode(level + 1, outs)
        received = swap(outs[1])
        own, received = outs[0][:each], received[:each]
        return jnp.concatenate(
            [jnp.where(core == 0, own, received), jnp.where(core == 0, received, own)], axis=1
        )

    return local


def solution(mesh):
    placed = (
        P(("member", "mesh"), "writer"),
        P(None, ("member", "mesh", "writer")),
        P("mesh", None, None, None),
        P("mesh", None),
        P("mesh", None),
        P("mesh"),
        P(),
        P(),
        P(),
        P(),
        P(),
    )
    return jax.shard_map(
        make_local(mesh.shape["mesh"]),
        mesh=mesh,
        in_specs=placed,
        out_specs=P("writer", ("member", "mesh")),
        check_vma=False,
    )
```

```python
import jax
import jax.numpy as jnp
from jax import lax
from jax.experimental import pallas as pl
from jax.experimental.pallas import tpu as pltpu
from jax.sharding import PartitionSpec as P

BLK = 128
K = 4
GROUP = 8
META = 5


def ring_order(count, columns):
    if columns == 1:
        return list(range(count))
    return list(range(0, count, 2)) + list(range(count - 1, 0, -2))


def prepare_kernel(count, columns, blocks, wanted, slots, live, order, w_out, b_out, state, w_in, nodes, interp, *rest):
    meta, heads, bias, ordered, w_in_kept, nodes_kept, interp_kept, entry_stage, sem = rest
    core = lax.axis_index("writer")
    tiles = live.shape[0] // 2
    first_tile = core * tiles
    pairs = [(w_in, w_in_kept), (nodes, nodes_kept)]
    eighth = max(tiles // 8, 1)
    for start in range(0, tiles, eighth):
        pairs.append((interp.at[pl.ds(first_tile + start, eighth)], interp_kept.at[pl.ds(start, eighth)]))
    kept = [pltpu.make_async_copy(source, target, sem.at[i]) for i, (source, target) in enumerate(pairs)]
    for copy in kept:
        copy.start()

    def place(index):
        if columns == 1:
            return index
        row = lax.shift_right_logical(index, 1)
        return jnp.where(lax.rem(index, 2) == 0, row, count - 1 - row)

    here = place(lax.axis_index("mesh"))
    first_stage = stages_of(count)[0]

    listed = wanted.shape[1]
    entry_work = tiles * META + len(levels_of(count)) * (tiles + 1)
    for stage in range(len(levels_of(count))):
        meta[tiles * META + stage * (tiles + 1)] = 0
        meta[entry_work + stage * (listed + 1)] = 0

    def locate(entry, _):
        block = wanted[0, entry]
        behind = here - place(lax.div(block, blocks))
        behind = jnp.where(core == 0, behind, -behind)
        behind = jnp.where(behind < 0, behind + count, behind)
        distance = jnp.minimum(behind, count - behind)
        stage = jnp.maximum(distance, first_stage) - first_stage
        far = count // 2
        if first_stage < far - 1:
            second = jnp.logical_or(distance == far, jnp.logical_and(distance == far - 1, behind > far))
            stage = stage + second.astype(jnp.int32)
        entry_stage[entry] = stage
        work = entry_work + stage * (listed + 1)
        meta[work] = meta[work] + 1
        code = behind * blocks + lax.rem(block, blocks)
        meta[work + meta[work]] = code * listed + entry
        return 0

    lax.fori_loop(0, listed, locate, 0)

    def describe(tile, _):
        number = first_tile + tile
        alive = live[number]
        stage = jnp.int32(0)
        for k in range(K):
            entry = slots[jnp.where(k < alive, k, 0), number]
            stage = jnp.maximum(stage, entry_stage[entry])
            meta[tile * META + k] = entry
        meta[tile * META + K] = alive
        work = tiles * META + stage * (tiles + 1)
        meta[work] = meta[work] + 1
        meta[work + meta[work]] = tile
        return 0

    lax.fori_loop(0, tiles, describe, 0)

    channels = state.shape[0]
    each = channels // 2
    rows = ordered.shape[0] // 2
    variable = lax.broadcasted_iota(jnp.int32, (channels, channels), 0)
    picks = jnp.where(variable == order[...], jnp.float32(1), jnp.float32(0)).T
    top, bottom = picks[:each], picks[each:]
    pad = jnp.zeros((rows - each, channels), jnp.float32)
    own, other = jnp.where(core == 0, top, bottom), jnp.where(core == 0, bottom, top)
    picks = jnp.concatenate([own, pad, other, pad], axis=0)
    bias[...] = jnp.sum(picks * b_out[...].astype(jnp.float32), axis=1, keepdims=True)
    picks = picks.astype(jnp.bfloat16)
    heads[...] = lax.dot_general(
        picks, w_out[...], (((1,), (0,)), ((), ())), preferred_element_type=jnp.float32
    ).astype(jnp.bfloat16)
    step = min(512, state.shape[1])
    for start in range(0, state.shape[1], step):
        part = jnp.dot(picks, state[:, start : start + step], preferred_element_type=jnp.float32)
        ordered[:, start : start + step] = part.astype(jnp.bfloat16)
    for copy in kept:
        copy.wait()


def in_hbm(array):
    return pltpu.with_memory_space_constraint(array, pltpu.HBM)


def prepare(count, columns, blocks, wanted, slots, live, order, w_out, b_out, state, w_in, nodes, interp):
    vmem, smem = pl.BlockSpec(memory_space=pltpu.VMEM), pl.BlockSpec(memory_space=pltpu.SMEM)
    rows = 2 * (-(-(state.shape[0] // 2) // 16) * 16)
    tiles = live.shape[0] // 2
    return pl.pallas_call(
        lambda *refs: prepare_kernel(count, columns, blocks, *refs),
        out_shape=[
            jax.ShapeDtypeStruct((tiles * META + len(levels_of(count)) * (tiles + wanted.shape[1] + 2),), jnp.int32),
            jax.ShapeDtypeStruct((rows, w_out.shape[1]), jnp.bfloat16),
            jax.ShapeDtypeStruct((rows, 1), jnp.float32),
            jax.ShapeDtypeStruct((rows, state.shape[1]), jnp.bfloat16),
            jax.ShapeDtypeStruct(w_in.shape, w_in.dtype),
            jax.ShapeDtypeStruct(nodes.shape, nodes.dtype),
            jax.ShapeDtypeStruct((tiles, *interp.shape[1:]), interp.dtype),
        ],
        in_specs=[smem] * 3 + [vmem] * 4 + [pl.BlockSpec(memory_space=pltpu.HBM)] * 3,
        out_specs=[smem] + [vmem] * 6,
        scratch_shapes=[pltpu.SMEM((wanted.shape[1],), jnp.int32), pltpu.SemaphoreType.DMA((2 + min(tiles, 8),))],
        compiler_params=pltpu.CompilerParams(vmem_limit_bytes=12 * 2**20),
        cost_estimate=pl.CostEstimate(flops=2 * rows * state.size, bytes_accessed=6 * state.size, transcendentals=0),
        name="prepare",
    )(*[in_hbm(x) for x in (wanted, slots, live, order, w_out, b_out, state, w_in, nodes, interp)])


def stages_of(count):
    far = count // 2
    return list(range(max(far - 3, 1), far + 1))


def levels_of(count):
    far, levels = count // 2, []
    for d in stages_of(count):
        if d == stages_of(count)[0]:
            levels.append([p for p in range(count) if min(p, count - p) <= d])
        elif d == far - 1:
            levels += [[d], [count - d]]
        else:
            levels.append(sorted({d, count - d}))
    return levels


def decode_kernel(stage, stages, blocks, pieces, tiles, held, *refs):
    meta, w_in, b_in, w_out, b_out, state, interp = refs[:7]
    piece_refs = refs[7 : 7 + 2 * len(pieces)]
    own_out, other_out, found = refs[7 + held + 2 * len(pieces) :]
    half = piece_refs[0].shape[1]
    rows = own_out.shape[0]
    listed = found.shape[0]
    core = lax.axis_index("writer")

    def columns_of(tile):
        return pl.ds(pl.multiple_of(tile * BLK, BLK), BLK)

    def take_block(code, entry, low, high):
        if high - low > 1:
            middle = (low + high) // 2
            below = code < pieces[middle] * blocks
            pl.when(below)(lambda: take_block(code, entry, low, middle))
            pl.when(jnp.logical_not(below))(lambda: take_block(code, entry, middle, high))
            return
        source = pl.ds(pl.multiple_of((code - pieces[low] * blocks) * BLK, BLK), BLK)
        for h in range(2):
            found[entry, :, h * half : (h + 1) * half] = piece_refs[2 * low + h][source, :]

    fresh = tiles * META + stages * (tiles + 1) + stage * (listed + 1)

    def take(i, _):
        packed = meta[fresh + 1 + i]
        take_block(lax.div(packed, listed), lax.rem(packed, listed), 0, len(pieces))
        return 0

    lax.fori_loop(0, meta[fresh], take, 0)

    work = tiles * META + stage * (tiles + 1)
    count = meta[work]

    def tile_at(i):
        return meta[work + 1 + i]

    def decode(first, size):
        aggregated = []
        for j in range(size):
            tile = tile_at(jnp.minimum(first + j, count - 1))
            live = meta[tile * META + K]
            spread = [interp[tile, k] for k in range(K)]
            spread = [a if k == 0 else jnp.where(k < live, a, jnp.zeros_like(a)) for k, a in enumerate(spread)]
            nodes = [found[meta[tile * META + k]] for k in range(K)]
            total = jnp.dot(
                jnp.concatenate(spread, axis=1), jnp.concatenate(nodes, axis=0), preferred_element_type=jnp.float32
            )
            aggregated.append(total.astype(jnp.bfloat16))
        aggregated = jnp.concatenate(aggregated, axis=0)
        layer = b_in[...].astype(jnp.float32)
        for h in range(2):
            features = pl.ds(pl.multiple_of((core if h == 0 else 1 - core) * half, half), half)
            layer = layer + jnp.dot(
                aggregated[:, h * half : (h + 1) * half], w_in[features, :], preferred_element_type=jnp.float32
            )
        hidden = (layer * (0.5 * jnp.tanh(0.5 * layer) + 0.5)).astype(jnp.bfloat16)
        decoded = lax.dot_general(
            w_out[...], hidden, (((1,), (1,)), ((), ())), preferred_element_type=jnp.float32
        )
        decoded = decoded + b_out[...]
        for j in range(size):
            tile = tile_at(jnp.minimum(first + j, count - 1))
            before = state[:, columns_of(tile)].astype(jnp.float32)
            after = (before + decoded[:, j * BLK : (j + 1) * BLK]).astype(jnp.bfloat16)
            own_out[:, columns_of(tile)] = after[:rows]
            other_out[:, columns_of(tile)] = after[rows:]

    def large(g, _):
        decode(g * GROUP, GROUP)
        return 0

    groups = count // GROUP
    lax.fori_loop(0, groups, large, 0)
    rest = count - groups * GROUP
    for size in range(2, GROUP + 1, 2):

        @pl.when(jnp.logical_and(rest > size - 2, rest <= size))
        def _():
            decode(groups * GROUP, size)


def decode_tiles(stage, stages, blocks, pieces, tiles, listed, small, arrays, outs):
    flat = [half for pair in arrays for half in pair]
    half = flat[0].shape[1]
    state = small[-2]
    rows = state.shape[0] // 2
    vmem = pl.BlockSpec(memory_space=pltpu.VMEM)
    first_out = 7 + len(flat)
    share = max(tiles // 4, 1)
    return pl.pallas_call(
        lambda *refs: decode_kernel(stage, stages, blocks, pieces, tiles, len(outs), *refs),
        out_shape=[jax.ShapeDtypeStruct((rows, state.shape[1]), jnp.bfloat16)] * 2
        + [jax.ShapeDtypeStruct((listed, BLK, 2 * half), jnp.bfloat16)],
        in_specs=[pl.BlockSpec(memory_space=pltpu.SMEM)] + [vmem] * (6 + len(flat) + len(outs)),
        out_specs=[vmem] * 3,
        input_output_aliases={first_out + j: j for j in range(len(outs))},
        compiler_params=pltpu.CompilerParams(vmem_limit_bytes=16 * 2**20),
        cost_estimate=pl.CostEstimate(
            flops=share * BLK * 2 * (K * BLK * 2 * half + 4 * half * half + 4 * half * rows),
            bytes_accessed=share * 6 * BLK * BLK * 10,
            transcendentals=share * BLK * 2 * half,
        ),
        name="decode_tiles",
    )(*small, *flat, *outs)


def make_local(count):
    columns = 2 if count == 8 else 1
    far = count // 2
    ring = ring_order(count, columns)
    onward = []
    for place in range(count):
        onward.append((ring[place] * 2, ring[(place + 1) % count] * 2))
        onward.append((ring[place] * 2 + 1, ring[(place - 1) % count] * 2 + 1))

    def send_on(piece):
        return lax.ppermute(piece, ("mesh", "writer"), onward)

    def swap(piece):
        return lax.ppermute(piece, "writer", [(0, 1), (1, 0)])

    def local(
        mesh_nodes,
        grid_state,
        interp,
        wanted,
        tile_slots,
        edge_count,
        w_in,
        b_in,
        w_out,
        b_out,
        writer_order,
    ):
        nodes = mesh_nodes.shape[0]
        blocks = nodes // BLK
        core = lax.axis_index("writer")
        tiles = interp.shape[0] // 2
        each = w_out.shape[1] // 2
        stages, levels = stages_of(count), levels_of(count)
        meta, heads, bias, state, w_in, nodes_kept, interp_kept = prepare(
            count,
            columns,
            blocks,
            wanted,
            tile_slots.T,
            edge_count,
            writer_order[None],
            w_out.T,
            b_out[None],
            grid_state,
            w_in,
            mesh_nodes,
            interp,
        )
        small = (meta, w_in, b_in[None], heads, bias, state, interp_kept)
        outs = []

        other_nodes = swap(mesh_nodes)
        same, cross = [mesh_nodes], [other_nodes]
        table = {0: (nodes_kept, other_nodes)}
        def decode(level, outs):
            pieces = levels[level]
            return list(
                decode_tiles(
                    level,
                    len(levels),
                    blocks,
                    pieces,
                    tiles,
                    wanted.shape[1],
                    small,
                    [table[p] for p in pieces],
                    outs,
                )
            )

        level = 0
        for d in range(1, far):
            if d == 2:
                same[-1], small = lax.optimization_barrier((same[-1], small))
            same.append(send_on(same[-1]))
            cross.append(send_on(cross[-1]))
            table[d] = (same[d], cross[d])
            swapped = (cross[d], same[d])
            if d - 1 in stages:
                outs, level = decode(level, outs), level + 1
                if d == far - 1:
                    last, outs = lax.optimization_barrier((same[d], outs))
                    outs, level = decode(level, outs), level + 1
                    first, outs = lax.optimization_barrier((cross[d], outs))
                    swapped = (first, last)
                else:
                    *swapped, outs = lax.optimization_barrier((*swapped, outs))
            table[count - d] = (swap(swapped[0]), swap(swapped[1]))
        same.append(send_on(same[-1]))
        outs = decode(level, outs)
        table[far] = (same[far], swap(same[far]))
        outs = decode(level + 1, outs)
        received = swap(outs[1])
        own, received = outs[0][:each], received[:each]
        return jnp.concatenate(
            [jnp.where(core == 0, own, received), jnp.where(core == 0, received, own)], axis=1
        )

    return local


def solution(mesh):
    placed = (
        P(("member", "mesh"), "writer"),
        P(None, ("member", "mesh", "writer")),
        P("mesh", None, None, None),
        P("mesh", None),
        P("mesh", None),
        P("mesh"),
        P(),
        P(),
        P(),
        P(),
        P(),
    )
    return jax.shard_map(
        make_local(mesh.shape["mesh"]),
        mesh=mesh,
        in_specs=placed,
        out_specs=P("writer", ("member", "mesh")),
        check_vma=False,
    )
```
